32 devices in a mesh: row: 4 (over y, x), col: 8 (over z, core).
Axes of the slice: x: 2, y: 2, z: 4, core: 2. Of those that a mesh axis runs over, the one named last changes fastest.
Arguments:
- a_tiles: bfloat16 [256, 16, 128, 128], P(('row', 'col')), may hold values from -0.5 to 0.5
- a_cols: int32 [256, 16], P(('row', 'col')), may hold values from -1 to 31, as said below
- p_tiles: bfloat16 [256, 2, 128, 128], P(('row', 'col')), may hold values from -0.375 to 0.375
- p_cols: int32 [256, 2], P(('row', 'col')), may hold values from 0 to 3, all different within a row
- send_list: int32 [32, 24], P(('row', 'col')), may hold values from 0 to 7
Outputs:
- coarse: float32 [2048, 1536], P(('row', 'col'))
The draws below stay inside these ranges and needn't reach their ends.
Inputs may be any that keep to these rules, and one draw needn't show every extreme that they name: a_cols is -1 for an empty slot, else an index below 32 into the buffer of step one; slot 0 of every block row is live and names the row itself; rows of the first row group never use t = 0 and rows of the last never t = 2; a device holds at most 80 live slots, and some device exactly 80. The 2 entries of a row of p_cols differ.
All inputs are finite; a program needn't handle non-finite values.
Results may differ from the reference program's by a relative error of at most 0.0029.
Values may be sent and summed in bfloat16 or wider, within the bound.
A program may use at most 64 MiB of HBM per device.

```python
import jax
import jax.numpy as jnp
from jax import lax

BS = 128
FB = 8
KA = 16
KP = 2
CG = 4
KLIVE = 80
NF = 256
N_ROW = 4
N_COL = 8


def draw_a_cols(key, part):
    device_total = N_ROW * N_COL
    slot_total = FB * KA
    spread = KLIVE - FB
    least_extra = spread * 5 // 9
    extra = jax.random.randint(jax.random.fold_in(key, 11), (device_total,), least_extra, spread + 1)
    busy_device = jax.random.randint(jax.random.fold_in(key, 13), (device_total,), 0, 8) == 0
    chosen = jax.random.randint(jax.random.fold_in(key, 14), (), 0, device_total)
    busy_device = busy_device | (jnp.arange(device_total, dtype=jnp.int32) == chosen)
    live_total = jnp.where(busy_device, KLIVE, FB + extra)
    scores = jax.random.randint(jax.random.fold_in(key, 15), (device_total, slot_total), 0, 2 ** 20)
    slot_pos = jnp.arange(slot_total, dtype=jnp.int32)
    is_diag = slot_pos % KA == 0
    sort_score = jnp.where(is_diag[None, :], -1, scores) * slot_total + slot_pos[None, :]
    ranking = jnp.argsort(jnp.argsort(sort_score, axis=1), axis=1)
    is_live = ranking < live_total[:, None]
    picked = jax.random.randint(jax.random.fold_in(key, 16), (device_total, slot_total), 0, FB + 3 * N_COL)
    group_of = jnp.arange(device_total, dtype=jnp.int32) // N_COL
    ghost_slot = jnp.maximum(picked - FB, 0)
    stream = ghost_slot % 3
    forbidden = (picked >= FB) & ((group_of[:, None] == 0) & (stream == 0) | (group_of[:, None] == N_ROW - 1) & (stream == 2))
    picked = jnp.where(forbidden, picked - stream + 1, picked)
    columns = jnp.where(is_diag[None, :], slot_pos[None, :] // KA, picked)
    columns = jnp.where(is_live, columns, -1)
    return columns.reshape(device_total * FB, KA).astype(jnp.int32)


def place_ends(drawn, key, low, top_value):
    index_at = [jax.random.randint(jax.random.fold_in(key, axis), (), 0, length) for axis, length in enumerate(drawn.shape)]
    longest = drawn.shape.index(max(drawn.shape))
    beside = index_at[:longest] + [(index_at[longest] + 1) % drawn.shape[longest]] + index_at[longest + 1:]
    return drawn.at[tuple(index_at)].set(low).at[tuple(beside)].set(top_value)


def block_levels(stream_key, dims, cuts, low, high):
    factor_of, own = 1.0, jax.random.fold_in(stream_key, 6)
    for position, blocks in cuts:
        heights = jnp.exp(jax.random.uniform(jax.random.fold_in(own, position), (blocks,), jnp.float32, low / len(cuts), high / len(cuts)))
        factor_of = factor_of * jnp.repeat(heights, dims[position] // blocks).reshape([-1 if axis == position else 1 for axis in range(len(dims))])
    return factor_of


def choose_distinct(stream_key, rows, amount, top, lift):
    order = jax.random.permutation(jax.random.fold_in(stream_key, 1), amount)
    favour = order
    for power in range(3):
        favour = favour * favour // amount
    favour = favour * lift // amount
    lots = jax.random.randint(jax.random.fold_in(stream_key, 2), (rows, amount), 0, 4096) + favour
    fixed_rows = jax.random.permutation(jax.random.fold_in(stream_key, 3), rows)[jnp.arange(amount) % rows]
    lots = jnp.where(jnp.arange(rows)[:, None] == fixed_rows[None, :], 1 << 14, lots)
    score = lots * amount + jnp.arange(amount)
    return lax.top_k(score.astype(jnp.int32), top)[1].astype(jnp.int32)


def gaussian(stream_key, shape, scale, most, split=(), kind=jnp.bfloat16):
    factor_of = block_levels(stream_key, shape, split, -0.22, 0.18) if split else 1.0
    array = jax.random.normal(stream_key, shape, jnp.float32) * scale * factor_of
    return jnp.minimum(jnp.maximum(array, -most), most).astype(kind)


def setup_inputs(seed: int = 0) -> dict:
    splits = jax.random.split(jax.random.key(seed), 6)
    return {
        "a_tiles": gaussian(splits[0], (NF, KA, BS, BS), BS ** -0.5, 0.5, ((0, 32),)),
        "a_cols": draw_a_cols(jax.random.fold_in(splits[5], 71), 0),
        "p_tiles": gaussian(splits[2], (NF, KP, BS, BS), (32 * FB) ** -0.5, 0.375, ((0, 32),)),
        "p_cols": choose_distinct(splits[3], NF, CG, KP, 0),
        "send_list": place_ends(jax.random.randint(splits[4], (N_ROW * N_COL, 3 * N_COL), 0, FB), jax.random.fold_in(splits[4], 1), 0, FB - 1).astype(jnp.int32),
    }


def reference(a_tiles, a_cols, p_tiles, p_cols, send_list):
    fine_total = FB * N_ROW * N_COL
    fine_index = jnp.arange(fine_total, dtype=jnp.int32)
    device_of = fine_index // FB
    group_of = device_of // N_COL
    column_of = device_of % N_COL
    is_live = a_cols >= 0
    buffer_slot = jnp.maximum(a_cols, 0)
    is_own = buffer_slot < FB
    ghost_slot = jnp.maximum(buffer_slot - FB, 0)
    source_col = ghost_slot // 3
    stream = ghost_slot % 3
    source_group = group_of[:, None] + stream - 1
    in_range = (source_group >= 0) & (source_group < N_ROW)
    source_device = jnp.clip(source_group, 0, N_ROW - 1) * N_COL + source_col
    listed = send_list[source_device, 3 * column_of[:, None] + stream]
    source_row = jnp.where(is_own, device_of[:, None] * FB + buffer_slot, source_device * FB + listed).astype(jnp.int32)
    weight = (is_live & (is_own | in_range)).astype(jnp.float32)
    offset = jnp.where(is_own, CG, stream * CG).astype(jnp.int32)
    window_ids = jnp.arange(3 * CG, dtype=jnp.int32)
    coarse_ids = jnp.arange(CG, dtype=jnp.int32)

    def group_sum(group):
        def add_block(coarse_acc, block):
            first_row = (group * N_COL + block) * FB
            rows_here = first_row + jnp.arange(FB, dtype=jnp.int32)
            a_block = a_tiles[rows_here].astype(jnp.float32)
            sources = source_row[rows_here]
            p_source = p_tiles[sources].astype(jnp.float32)
            rel_col = offset[rows_here][:, :, None] + p_cols[sources]
            member = (rel_col[..., None] == window_ids).astype(jnp.float32) * weight[rows_here][:, :, None, None]
            tile_prod = jnp.einsum("rkxy,rkpyz->rkpxz", a_block, p_source)
            placed = jnp.einsum("rkpl,rkpxz->rxlz", member, tile_prod)
            product_rows = placed.reshape(FB * BS, 3 * CG * BS).astype(jnp.bfloat16)
            own_member = (p_cols[rows_here][..., None] == coarse_ids).astype(jnp.float32)
            dense_prolong = jnp.einsum("rpm,rpxy->rxmy", own_member, p_tiles[rows_here].astype(jnp.float32))
            dense_prolong = dense_prolong.reshape(FB * BS, CG * BS).astype(jnp.bfloat16)
            update = jnp.dot(dense_prolong.T, product_rows, preferred_element_type=jnp.float32)
            return coarse_acc + update, None

        start_acc = jnp.zeros((CG * BS, 3 * CG * BS), jnp.float32)
        result, unused = lax.scan(add_block, start_acc, jnp.arange(N_COL, dtype=jnp.int32))
        return result

    groups = lax.map(group_sum, jnp.arange(N_ROW, dtype=jnp.int32))
    return groups.reshape(N_ROW * CG * BS, 3 * CG * BS)
```

```python
import functools

import jax
import jax.numpy as jnp
from jax import lax
from jax.experimental import pallas as pl
from jax.experimental.pallas import tpu as pltpu
from jax.sharding import PartitionSpec as P

CG = 4
MESH = pl.DeviceIdType.MESH
UNROLL = 4
VMEM_LIMIT = 48 * 1024 * 1024


def far_first(index, count, step):
    half = count // 2
    side, local = index // half, index % half
    other = step < half
    side = jnp.where(other, 1 - side, side)
    return side * half + (local + step) % half


def exchange_kernel(
    row_count, col_count, p_ref, pc_ref, sl_ref, buf_ref, cols_ref,
    send, send_cols, tile_ss, tile_rs, cols_ss, cols_rs,
):
    g, c = lax.axis_index("row"), lax.axis_index("col")
    own = p_ref.shape[0]
    bs = p_ref.shape[-1]

    def group_ok(group):
        return (group >= 0) & (group < row_count)

    barrier = pltpu.get_barrier_semaphore()

    @pl.loop(0, col_count)
    def _(other):
        for t in range(3):
            group = g + 1 - t

            @pl.when(group_ok(group) & ((other != c) | (t != 1)))
            def _():
                pl.semaphore_signal(barrier, inc=1, device_id=(group, other), device_id_type=MESH)

    lane = lax.broadcasted_iota(jnp.int32, (1, bs), 1)

    @pl.loop(0, col_count)
    def _(other):
        for t in range(3):
            j = other * 3 + t
            r = sl_ref[0, j]
            send[j, :, 0:bs] = p_ref[r, 0]
            send[j, :, bs : 2 * bs] = p_ref[r, 1]
            send_cols[j] = jnp.where(lane == 0, pc_ref[r, 0], pc_ref[r, 1]) + t * CG

    peers = col_count - 1
    peers = peers + jnp.where(g > 0, col_count, 0) + jnp.where(g < row_count - 1, col_count, 0)
    pl.semaphore_wait(barrier, peers)

    def tiles_copy(source, target, group, other):
        return pltpu.make_async_remote_copy(
            src_ref=send.at[source], dst_ref=buf_ref.at[own + target],
            send_sem=tile_ss.at[source], recv_sem=tile_rs.at[target],
            device_id=(group, other), device_id_type=MESH,
        )

    def cols_copy(source, target, group, other):
        return pltpu.make_async_remote_copy(
            src_ref=send_cols.at[source], dst_ref=cols_ref.at[own + target],
            send_sem=cols_ss.at[source], recv_sem=cols_rs.at[target],
            device_id=(group, other), device_id_type=MESH,
        )

    @pl.loop(0, col_count)
    def _(step):
        other = far_first(c, col_count, step)
        for t in range(3):
            group = g + 1 - t

            @pl.when(group_ok(group) & ((other != c) | (t != 1)))
            def _():
                tiles_copy(other * 3 + t, c * 3 + t, group, other).start()
                cols_copy(other * 3 + t, c * 3 + t, group, other).start()

    @pl.loop(0, own)
    def _(r):
        buf_ref[r, :, 0:bs] = p_ref[r, 0]
        buf_ref[r, :, bs : 2 * bs] = p_ref[r, 1]
        cols_ref[r] = jnp.where(lane == 0, pc_ref[r, 0], pc_ref[r, 1]) + CG

    mine = c * 3 + 1
    buf_ref[own + mine] = send[mine]
    cols_ref[own + mine] = send_cols[mine]

    @pl.loop(0, col_count)
    def _(other):
        for t in range(3):
            slot = other * 3 + t
            not_self = (other != c) | (t != 1)

            @pl.when(group_ok(g + 1 - t) & not_self)
            def _():
                tiles_copy(slot, slot, g + 1 - t, other).wait_send()
                cols_copy(slot, slot, g + 1 - t, other).wait_send()

            @pl.when(group_ok(g + t - 1) & not_self)
            def _():
                tiles_copy(slot, slot, g + t - 1, other).wait_recv()
                cols_copy(slot, slot, g + t - 1, other).wait_recv()


def product_kernel(
    col_count, acols_ref, pc_ref, cols_ref, a_ref, p_ref, buf_ref, prod_ref, dpt_ref,
    acc, slot_of, src_of, to_first, to_second,
):
    rows, slots = acols_ref.shape
    bs = a_ref.shape[-1]
    window = 3 * CG
    dump = rows * window

    def collect(s, count):
        i = s // slots
        b = acols_ref[i, s % slots]
        src = jnp.maximum(b, 0)
        slot_of[count] = s
        src_of[count] = src
        to_first[count] = i * window + cols_ref[src, 0, 0]
        to_second[count] = i * window + cols_ref[src, 0, 1]
        return count + (b >= 0).astype(jnp.int32)

    live = lax.fori_loop(0, rows * slots, collect, jnp.int32(0))
    for extra in range(UNROLL):
        slot_of[live + extra] = 0
        src_of[live + extra] = 0
        to_first[live + extra] = dump
        to_second[live + extra] = dump

    @pl.loop(0, rows)
    def _(i):
        acc[pl.ds(i * window, window)] = jnp.zeros((window, bs, bs), jnp.float32)

    dpt_ref[...] = jnp.zeros_like(dpt_ref)
    owners = col_count // CG
    piece = bs // owners
    half = CG * bs // 2
    for i in range(rows):
        for p in range(p_ref.shape[1]):
            flipped = p_ref[i, p].astype(jnp.float32).T.astype(jnp.bfloat16)
            m = pc_ref[i, p]
            for u in range(owners):
                start = (u % 2) * half + (m * (owners // 2) + u // 2) * piece
                dpt_ref[pl.ds(pl.multiple_of(start, piece), piece), i * bs : (i + 1) * bs] = (
                    flipped[u * piece : (u + 1) * piece]
                )

    @pl.loop(0, (live + UNROLL - 1) // UNROLL)
    def _(step):
        first = step * UNROLL
        outs = [
            jnp.dot(a_ref[slot_of[first + u]], buf_ref[src_of[first + u]], preferred_element_type=jnp.float32)
            for u in range(UNROLL)
        ]
        for u in range(UNROLL):
            acc[to_first[first + u]] += outs[u][:, :bs]
            acc[to_second[first + u]] += outs[u][:, bs:]

    @pl.loop(0, rows)
    def _(i):
        for l in range(window):
            prod_ref[pl.ds(pl.multiple_of(i * bs, bs), bs), l * bs : (l + 1) * bs] = acc[
                i * window + l
            ].astype(jnp.bfloat16)


def reduce_kernel(
    col_count, dpt_ref, prod_ref, out_ref, pair_send, pair_recv, kept, line_send, line_recv,
    pair_ss, pair_rs, line_ss, line_rs,
):
    g, c = lax.axis_index("row"), lax.axis_index("col")
    chips = col_count // 2
    z, k = c // 2, c % 2
    piece, width = out_ref.shape
    half = chips * piece
    chunk = 512

    barrier = pltpu.get_barrier_semaphore()
    pl.semaphore_signal(barrier, inc=1, device_id=(g, 2 * z + 1 - k), device_id_type=MESH)

    @pl.loop(1, chips)
    def _(step):
        other = (z + step) % chips
        pl.semaphore_signal(barrier, inc=1, device_id=(g, 2 * other + k), device_id_type=MESH)

    def multiply(core, target):
        rows = dpt_ref[pl.ds(pl.multiple_of(core * half, half), half), :]
        for n in range(0, width, chunk):
            part = jnp.dot(rows, prod_ref[:, n : n + chunk], preferred_element_type=jnp.float32)
            for s in range(chips):
                target[s, :, n : n + chunk] = part[s * piece : (s + 1) * piece]

    multiply(1 - k, pair_send)
    pl.semaphore_wait(barrier, chips)

    def pair_copy(s):
        return pltpu.make_async_remote_copy(
            src_ref=pair_send.at[s], dst_ref=pair_recv.at[s],
            send_sem=pair_ss.at[s], recv_sem=pair_rs.at[s],
            device_id=(g, 2 * z + 1 - k), device_id_type=MESH,
        )

    def line_copy(source, target, other):
        return pltpu.make_async_remote_copy(
            src_ref=line_send.at[source], dst_ref=line_recv.at[target],
            send_sem=line_ss.at[source], recv_sem=line_rs.at[target],
            device_id=(g, 2 * other + k), device_id_type=MESH,
        )

    @pl.loop(0, chips)
    def _(step):
        pair_copy(far_first(z, chips, step)).start()

    multiply(k, kept)

    @pl.loop(0, chips)
    def _(step):
        other = far_first(z, chips, step)
        pair_copy(other).wait_recv()

        @pl.when(other != z)
        def _():
            line_send[other] = (kept[other] + pair_recv[other]).astype(jnp.bfloat16)
            line_copy(other, z, other).start()

        @pl.when(other == z)
        def _():
            out_ref[...] = kept[other] + pair_recv[other]

    @pl.loop(1, chips)
    def _(step):
        other = (z + step) % chips
        line_copy(other, other, other).wait_recv()
        out_ref[...] += line_recv[other].astype(jnp.float32)
        line_copy(other, other, other).wait_send()

    @pl.loop(0, chips)
    def _(s):
        pair_copy(s).wait_send()


def body(row_count, col_count, a_tiles, a_cols, p_tiles, p_cols, send_list):
    own, slots = a_cols.shape
    tiles = p_cols.shape[1]
    bs = a_tiles.shape[-1]
    ghosts = 3 * col_count
    window = 3 * CG
    vmem = pl.BlockSpec(memory_space=pltpu.VMEM)
    smem = pl.BlockSpec(memory_space=pltpu.SMEM)
    dma = pltpu.SemaphoreType.DMA
    buffer_tiles, buffer_cols = pl.pallas_call(
        functools.partial(exchange_kernel, row_count, col_count),
        out_shape=(
            jax.ShapeDtypeStruct((own + ghosts, bs, tiles * bs), jnp.bfloat16),
            jax.ShapeDtypeStruct((own + ghosts, 1, bs), jnp.int32),
        ),
        in_specs=[vmem, smem, smem],
        out_specs=(vmem, vmem),
        scratch_shapes=[
            pltpu.VMEM((ghosts, bs, tiles * bs), jnp.bfloat16),
            pltpu.VMEM((ghosts, 1, bs), jnp.int32),
            dma((ghosts,)), dma((ghosts,)), dma((ghosts,)), dma((ghosts,)),
        ],
        compiler_params=pltpu.CompilerParams(
            collective_id=0, has_side_effects=True, vmem_limit_bytes=VMEM_LIMIT
        ),
        name="exchange",
    )(p_tiles, p_cols, send_list)
    room = own * slots + UNROLL
    product_rows, prolong_t = pl.pallas_call(
        functools.partial(product_kernel, col_count),
        out_shape=(
            jax.ShapeDtypeStruct((own * bs, window * bs), jnp.bfloat16),
            jax.ShapeDtypeStruct((CG * bs, own * bs), jnp.bfloat16),
        ),
        in_specs=[smem, smem, smem, vmem, vmem, vmem],
        out_specs=(vmem, vmem),
        scratch_shapes=[pltpu.VMEM((own * window + 1, bs, bs), jnp.float32)]
        + [pltpu.SMEM((room,), jnp.int32)] * 4,
        compiler_params=pltpu.CompilerParams(vmem_limit_bytes=VMEM_LIMIT),
        name="product",
    )(
        a_cols, p_cols, buffer_cols[:, :, :tiles],
        a_tiles.reshape(own * slots, bs, bs), p_tiles, buffer_tiles,
    )
    chips = col_count // 2
    piece = CG * bs // col_count
    blocks = (chips, piece, window * bs)
    return pl.pallas_call(
        functools.partial(reduce_kernel, col_count),
        out_shape=jax.ShapeDtypeStruct((piece, window * bs), jnp.float32),
        in_specs=[vmem, vmem],
        out_specs=vmem,
        scratch_shapes=[
            pltpu.VMEM(blocks, jnp.float32),
            pltpu.VMEM(blocks, jnp.float32),
            pltpu.VMEM(blocks, jnp.float32),
            pltpu.VMEM(blocks, jnp.bfloat16),
            pltpu.VMEM(blocks, jnp.bfloat16),
            dma((chips,)), dma((chips,)), dma((chips,)), dma((chips,)),
        ],
        compiler_params=pltpu.CompilerParams(
            collective_id=1, has_side_effects=True, vmem_limit_bytes=VMEM_LIMIT
        ),
        name="reduce",
    )(prolong_t, product_rows)


def solution(mesh):
    in_specs = (
        P(("row", "col"), None, None, None),
        P(("row", "col"), None),
        P(("row", "col"), None, None, None),
        P(("row", "col"), None),
        P(("row", "col"), None),
    )
    out_specs = P(("row", "col"), None)
    return jax.shard_map(
        functools.partial(body, mesh.shape["row"], mesh.shape["col"]),
        mesh=mesh, in_specs=in_specs, out_specs=out_specs, check_vma=False,
    )
```

```python
import functools

import jax
import jax.numpy as jnp
from jax import lax
from jax.experimental import pallas as pl
from jax.experimental.pallas import tpu as pltpu
from jax.sharding import PartitionSpec as P

CG = 4
MESH = pl.DeviceIdType.MESH
ORDER = (1, 0, 2)
VMEM_LIMIT = 56 * 1024 * 1024


def far_first(index, count, step):
    half = count // 2
    side, local = index // half, index % half
    side = jnp.where(step < half, 1 - side, side)
    return side * half + (local + step) % half


def kernel(
    row_count, col_count, a_hbm, p_ref, ac_ref, pc_ref, sl_ref, out_ref,
    a_vm, send, send_cols, recv, recv_cols, dense, rt, prod,
    pair_send, pair_recv, kept, line_send, line_recv,
    a_sem, tile_ss, tile_rs, cols_ss, cols_rs, pair_ss, pair_rs, line_ss, line_rs,
):
    g, c = lax.axis_index("row"), lax.axis_index("col")
    chips = col_count // 2
    z, k = c // 2, c % 2
    own, slots = ac_ref.shape
    bs = p_ref.shape[-1]
    ghosts = 3 * col_count
    zero_row = own + ghosts
    wide = CG * bs
    piece = wide // col_count
    half = wide // 2
    f32, bf16 = jnp.float32, jnp.bfloat16

    def group_ok(group):
        return (group >= 0) & (group < row_count)

    def a_copy(s):
        return pltpu.make_async_copy(
            a_hbm.at[:, s], a_vm.at[:, :, pl.ds(s * bs, bs)], a_sem.at[s]
        )

    barrier = pltpu.get_barrier_semaphore()

    @pl.loop(0, col_count)
    def _(other):
        for t in range(3):
            group = g + 1 - t

            @pl.when(group_ok(group) & ((other != c) | (t != 1)))
            def _():
                pl.semaphore_signal(barrier, inc=1, device_id=(group, other), device_id_type=MESH)

    for s in range(slots):
        a_copy(s).start()

    def pattern(r):
        lane = lax.broadcasted_iota(jnp.int32, (1, 2 * bs), 1)
        return jnp.where(lane < bs, pc_ref[r, 0], pc_ref[r, 1])

    @pl.loop(0, col_count)
    def _(other):
        for t in range(3):
            j = other * 3 + t
            r = sl_ref[0, j]
            send[j, 0] = p_ref[r, 0]
            send[j, 1] = p_ref[r, 1]
            send_cols[j] = pattern(r)

    peers = col_count - 1
    peers = peers + jnp.where(g > 0, col_count, 0) + jnp.where(g < row_count - 1, col_count, 0)
    pl.semaphore_wait(barrier, peers)

    def tiles_copy(source, target, group, other):
        return pltpu.make_async_remote_copy(
            src_ref=send.at[source], dst_ref=recv.at[target],
            send_sem=tile_ss.at[source], recv_sem=tile_rs.at[target],
            device_id=(group, other), device_id_type=MESH,
        )

    def cols_copy(source, target, group, other):
        return pltpu.make_async_remote_copy(
            src_ref=send_cols.at[source], dst_ref=recv_cols.at[target],
            send_sem=cols_ss.at[source], recv_sem=cols_rs.at[target],
            device_id=(group, other), device_id_type=MESH,
        )

    def pair_copy(w):
        return pltpu.make_async_remote_copy(
            src_ref=pair_send.at[w], dst_ref=pair_recv.at[w],
            send_sem=pair_ss.at[w], recv_sem=pair_rs.at[w],
            device_id=(g, 2 * z + 1 - k), device_id_type=MESH,
        )

    def line_copy(w, source, target, other):
        return pltpu.make_async_remote_copy(
            src_ref=line_send.at[w, source], dst_ref=line_recv.at[w, target],
            send_sem=line_ss.at[w, source], recv_sem=line_rs.at[w, target],
            device_id=(g, 2 * other + k), device_id_type=MESH,
        )

    for t in ORDER:
        group = g + 1 - t

        @pl.loop(0, col_count)
        def _(step):
            other = far_first(c, col_count, step)

            @pl.when(group_ok(group) & ((other != c) | (t != 1)))
            def _():
                cols_copy(other * 3 + t, c * 3 + t, group, other).start()
                tiles_copy(other * 3 + t, c * 3 + t, group, other).start()

    def spread(target, tiles, cols):
        first, second = tiles[0].astype(f32), tiles[1].astype(f32)
        for m in range(CG):
            in_first = jnp.where(cols[:, :bs] == m, 1.0, 0.0)
            in_second = jnp.where(cols[:, bs:] == m, 1.0, 0.0)
            dense[target, :, m * bs : (m + 1) * bs] = (
                first * in_first + second * in_second
            ).astype(bf16)

    dense[zero_row] = jnp.zeros((bs, wide), bf16)
    owners = col_count // CG

    @pl.loop(0, own)
    def _(r):
        spread(r, p_ref.at[r], pattern(r))
        first = p_ref[r, 0].astype(f32).T
        second = p_ref[r, 1].astype(f32).T
        for m in range(CG):
            in_first = jnp.where(pc_ref[r, 0] == m, 1.0, 0.0)
            in_second = jnp.where(pc_ref[r, 1] == m, 1.0, 0.0)
            block = (first * in_first + second * in_second).astype(bf16)
            for u in range(owners):
                start = (u % 2) * half + (m * (owners // 2) + u // 2) * piece
                rt[start : start + piece, pl.ds(pl.multiple_of(r * bs, bs), bs)] = block[
                    u * piece : (u + 1) * piece
                ]

    def take_stream(t):
        @pl.loop(0, col_count)
        def _(other):
            slot = other * 3 + t

            @pl.when(group_ok(g + t - 1) & ((other != c) | (t != 1)))
            def _():
                cols_copy(slot, slot, g + t - 1, other).wait_recv()
                tiles_copy(slot, slot, g + t - 1, other).wait_recv()
                spread(own + slot, recv.at[slot], recv_cols[slot])

            if t == 1:

                @pl.when(other == c)
                def _():
                    spread(own + slot, send.at[slot], send_cols[slot])

    def products(w):
        @pl.loop(0, own)
        def _(i):
            index = []
            for s in range(slots):
                b = ac_ref[i, s]
                ghost = jnp.maximum(b - own, 0)
                stream = jnp.where(b < own, 1, ghost % 3)
                index.append(jnp.where((b >= 0) & (stream == w), b, zero_row))
            for n in range(0, wide, 2 * bs):
                total = jnp.zeros((bs, 2 * bs), f32)
                for s in range(0, slots, 2):
                    right = jnp.concatenate(
                        [dense[index[s], :, n : n + 2 * bs], dense[index[s + 1], :, n : n + 2 * bs]],
                        axis=0,
                    )
                    left = a_vm[i, :, s * bs : (s + 2) * bs]
                    total = total + jnp.dot(left, right, preferred_element_type=f32)
                prod[pl.ds(pl.multiple_of(i * bs, bs), bs), n : n + 2 * bs] = total.astype(bf16)

    def restrict(core):
        rows = rt[pl.ds(pl.multiple_of(core * half, half), half), :]
        return jnp.dot(rows, prod[...], preferred_element_type=f32)

    def line_stage(w):
        pair_copy(w).wait_recv()
        columns = slice(w * wide, (w + 1) * wide)

        @pl.loop(0, chips)
        def _(step):
            other = far_first(z, chips, step)
            rows = pl.ds(pl.multiple_of(other * piece, piece), piece)

            @pl.when(other != z)
            def _():
                line_send[w, other] = (kept[w, rows] + pair_recv[w, rows]).astype(bf16)
                line_copy(w, other, z, other).start()

            @pl.when(other == z)
            def _():
                out_ref[:, columns] = kept[w, rows] + pair_recv[w, rows]

    for s in range(slots):
        a_copy(s).wait()
    for n, w in enumerate(ORDER):
        take_stream(w)
        if n == 2:
            line_stage(ORDER[0])
            line_stage(ORDER[1])
        products(w)
        pair_send[w] = restrict(1 - k)
        pair_copy(w).start()
        kept[w] = restrict(k)
    line_stage(ORDER[2])

    for w in ORDER:
        columns = slice(w * wide, (w + 1) * wide)

        @pl.loop(1, chips)
        def _(step):
            other = (z + step) % chips
            line_copy(w, other, other, other).wait_recv()
            out_ref[:, columns] += line_recv[w, other].astype(f32)
            line_copy(w, other, other, other).wait_send()

        pair_copy(w).wait_send()

        @pl.loop(0, col_count)
        def _(other):
            slot = other * 3 + w

            @pl.when(group_ok(g + 1 - w) & ((other != c) | (w != 1)))
            def _():
                cols_copy(slot, slot, g + 1 - w, other).wait_send()
                tiles_copy(slot, slot, g + 1 - w, other).wait_send()


def body(row_count, col_count, a_tiles, a_cols, p_tiles, p_cols, send_list):
    own, slots = a_cols.shape
    tiles = p_cols.shape[1]
    bs = a_tiles.shape[-1]
    ghosts = 3 * col_count
    chips = col_count // 2
    wide = CG * bs
    piece = wide // col_count
    vmem = pl.BlockSpec(memory_space=pltpu.VMEM)
    smem = pl.BlockSpec(memory_space=pltpu.SMEM)
    dma = pltpu.SemaphoreType.DMA
    f32, bf16 = jnp.float32, jnp.bfloat16
    return pl.pallas_call(
        functools.partial(kernel, row_count, col_count),
        out_shape=jax.ShapeDtypeStruct((piece, 3 * wide), f32),
        in_specs=[pl.BlockSpec(memory_space=pl.ANY), vmem, smem, smem, smem],
        out_specs=vmem,
        scratch_shapes=[
            pltpu.VMEM((own, bs, slots * bs), bf16),
            pltpu.VMEM((ghosts, tiles, bs, bs), bf16),
            pltpu.VMEM((ghosts, 1, tiles * bs), jnp.int32),
            pltpu.VMEM((ghosts, tiles, bs, bs), bf16),
            pltpu.VMEM((ghosts, 1, tiles * bs), jnp.int32),
            pltpu.VMEM((own + ghosts + 1, bs, wide), bf16),
            pltpu.VMEM((wide, own * bs), bf16),
            pltpu.VMEM((own * bs, wide), bf16),
            pltpu.VMEM((3, wide // 2, wide), f32),
            pltpu.VMEM((3, wide // 2, wide), f32),
            pltpu.VMEM((3, wide // 2, wide), f32),
            pltpu.VMEM((3, chips, piece, wide), bf16),
            pltpu.VMEM((3, chips, piece, wide), bf16),
            dma((slots,)),
            dma((ghosts,)), dma((ghosts,)), dma((ghosts,)), dma((ghosts,)),
            dma((3,)), dma((3,)), dma((3, chips)), dma((3, chips)),
        ],
        compiler_params=pltpu.CompilerParams(
            collective_id=0, has_side_effects=True, vmem_limit_bytes=VMEM_LIMIT
        ),
        name="triple_product",
    )(a_tiles, p_tiles, a_cols, p_cols, send_list)


def solution(mesh):
    in_specs = (
        P(("row", "col"), None, None, None),
        P(("row", "col"), None),
        P(("row", "col"), None, None, None),
        P(("row", "col"), None),
        P(("row", "col"), None),
    )
    out_specs = P(("row", "col"), None)
    return jax.shard_map(
        functools.partial(body, mesh.shape["row"], mesh.shape["col"]),
        mesh=mesh, in_specs=in_specs, out_specs=out_specs, check_vma=False,
    )
```

```python
import functools

import jax
import jax.numpy as jnp
from jax import lax
from jax.experimental import pallas as pl
from jax.experimental.pallas import tpu as pltpu
from jax.sharding import PartitionSpec as P

CG = 4
MESH = pl.DeviceIdType.MESH
ORDER = (1, 0, 2)
VMEM_LIMIT = 56 * 1024 * 1024


def far_first(index, count, step):
    half = count // 2
    side, local = index // half, index % half
    side = jnp.where(step < half, 1 - side, side)
    return side * half + (local + step) % half


def kernel(
    row_count, col_count, a_hbm, p_ref, ac_ref, pc_ref, sl_ref, out_ref,
    a_vm, send, send_cols, recv, recv_cols, dense, rt, prod,
    pair_send, pair_recv, kept, line_send, combo, line_recv,
    a_sem, tile_ss, tile_rs, cols_ss, cols_rs, pair_ss, pair_rs, line_ss, combo_rs, line_rs,
):
    g, c = lax.axis_index("row"), lax.axis_index("col")
    chips = col_count // 2
    z, k = c // 2, c % 2
    own, slots = ac_ref.shape
    bs = p_ref.shape[-1]
    ghosts = 3 * col_count
    zero_row = own + ghosts
    wide = CG * bs
    piece = wide // col_count
    half = wide // 2
    couple = z // 2
    buddy = z + 1 - 2 * (z % 2)
    f32, bf16 = jnp.float32, jnp.bfloat16

    def group_ok(group):
        return (group >= 0) & (group < row_count)

    def a_copy(s):
        return pltpu.make_async_copy(
            a_hbm.at[:, s], a_vm.at[:, :, pl.ds(s * bs, bs)], a_sem.at[s]
        )

    barrier = pltpu.get_barrier_semaphore()

    @pl.loop(0, col_count)
    def _(other):
        for t in range(3):
            group = g + 1 - t

            @pl.when(group_ok(group) & ((other != c) | (t != 1)))
            def _():
                pl.semaphore_signal(barrier, inc=1, device_id=(group, other), device_id_type=MESH)

    for s in range(slots):
        a_copy(s).start()

    def pattern(r):
        lane = lax.broadcasted_iota(jnp.int32, (1, 2 * bs), 1)
        return jnp.where(lane < bs, pc_ref[0, r], pc_ref[1, r])

    @pl.loop(0, col_count)
    def _(other):
        for t in range(3):
            j = other * 3 + t
            r = sl_ref[0, j]
            send[j, 0] = p_ref[r, 0]
            send[j, 1] = p_ref[r, 1]
            send_cols[j] = pattern(r)

    peers = col_count - 1
    peers = peers + jnp.where(g > 0, col_count, 0) + jnp.where(g < row_count - 1, col_count, 0)
    pl.semaphore_wait(barrier, peers)

    def tiles_copy(source, target, group, other):
        return pltpu.make_async_remote_copy(
            src_ref=send.at[source], dst_ref=recv.at[target],
            send_sem=tile_ss.at[source], recv_sem=tile_rs.at[target],
            device_id=(group, other), device_id_type=MESH,
        )

    def cols_copy(source, target, group, other):
        return pltpu.make_async_remote_copy(
            src_ref=send_cols.at[source], dst_ref=recv_cols.at[target],
            send_sem=cols_ss.at[source], recv_sem=cols_rs.at[target],
            device_id=(group, other), device_id_type=MESH,
        )

    def pair_copy(w):
        return pltpu.make_async_remote_copy(
            src_ref=pair_send.at[w], dst_ref=pair_recv.at[w],
            send_sem=pair_ss.at[w], recv_sem=pair_rs.at[w],
            device_id=(g, 2 * z + 1 - k), device_id_type=MESH,
        )

    def line_copy(w, block, target, other):
        return pltpu.make_async_remote_copy(
            src_ref=line_send.at[w, block], dst_ref=line_recv.at[w, target],
            send_sem=line_ss.at[w, block], recv_sem=line_rs.at[w, target],
            device_id=(g, 2 * other + k), device_id_type=MESH,
        )

    def combo_copy(w, block):
        return pltpu.make_async_remote_copy(
            src_ref=line_send.at[w, block], dst_ref=combo.at[w, block],
            send_sem=line_ss.at[w, block], recv_sem=combo_rs.at[w, block],
            device_id=(g, 2 * buddy + k), device_id_type=MESH,
        )

    for t in ORDER:
        group = g + 1 - t

        @pl.loop(0, col_count)
        def _(step):
            other = far_first(c, col_count, step)

            @pl.when(group_ok(group) & ((other != c) | (t != 1)))
            def _():
                cols_copy(other * 3 + t, c * 3 + t, group, other).start()
                tiles_copy(other * 3 + t, c * 3 + t, group, other).start()

    def spread(target, tiles, cols):
        first, second = tiles[0].astype(f32), tiles[1].astype(f32)
        for m in range(CG):
            in_first = jnp.where(cols[:, :bs] == m, 1.0, 0.0)
            in_second = jnp.where(cols[:, bs:] == m, 1.0, 0.0)
            dense[target, :, m * bs : (m + 1) * bs] = (
                first * in_first + second * in_second
            ).astype(bf16)

    dense[zero_row] = jnp.zeros((bs, wide), bf16)
    owners = col_count // CG

    @pl.loop(0, own)
    def _(r):
        spread(r, p_ref.at[r], pattern(r))
        first = p_ref[r, 0].astype(f32).T
        second = p_ref[r, 1].astype(f32).T
        for m in range(CG):
            in_first = jnp.where(pc_ref[0, r] == m, 1.0, 0.0)
            in_second = jnp.where(pc_ref[1, r] == m, 1.0, 0.0)
            block = (first * in_first + second * in_second).astype(bf16)
            for u in range(owners):
                start = (u % 2) * half + (m * (owners // 2) + u // 2) * piece
                rt[start : start + piece, pl.ds(pl.multiple_of(r * bs, bs), bs)] = block[
                    u * piece : (u + 1) * piece
                ]

    def take_stream(t):
        @pl.loop(0, col_count)
        def _(other):
            slot = other * 3 + t

            @pl.when(group_ok(g + t - 1) & ((other != c) | (t != 1)))
            def _():
                cols_copy(slot, slot, g + t - 1, other).wait_recv()
                tiles_copy(slot, slot, g + t - 1, other).wait_recv()
                spread(own + slot, recv.at[slot], recv_cols[slot])

            if t == 1:

                @pl.when(other == c)
                def _():
                    spread(own + slot, send.at[slot], send_cols[slot])

    def products(w, low, high):
        @pl.loop(low, high)
        def _(i):
            index = []
            for s in range(slots):
                b = ac_ref[i, s]
                ghost = jnp.maximum(b - own, 0)
                stream = jnp.where(b < own, 1, ghost % 3)
                index.append(jnp.where((b >= 0) & (stream == w), b, zero_row))
            for n in range(0, wide, 2 * bs):
                total = jnp.zeros((bs, 2 * bs), f32)
                for s in range(0, slots, 2):
                    right = jnp.concatenate(
                        [dense[index[s], :, n : n + 2 * bs], dense[index[s + 1], :, n : n + 2 * bs]],
                        axis=0,
                    )
                    left = a_vm[i, :, s * bs : (s + 2) * bs]
                    total = total + jnp.dot(left, right, preferred_element_type=f32)
                prod[pl.ds(pl.multiple_of(i * bs, bs), bs), n : n + 2 * bs] = total.astype(bf16)

    def restrict(core):
        rows = rt[pl.ds(pl.multiple_of(core * half, half), half), :]
        return jnp.dot(rows, prod[...], preferred_element_type=f32)

    def block_rows(other):
        return pl.ds(pl.multiple_of(other * piece, piece), piece)

    def beyond_buddy(other):
        return jnp.where(z % 2 == 0, other > z + 1, other < z - 1)

    def beyond_self(other):
        return jnp.where(z % 2 == 0, other < z, other > z)

    def give(w):
        pair_copy(w).wait_recv()
        kept[w] = kept[w] + pair_recv[w]
        out_ref[:, w * wide : (w + 1) * wide] = kept[w, block_rows(z)]

        @pl.loop(0, chips)
        def _(step):
            other = far_first(z, chips, step)

            @pl.when(beyond_buddy(other))
            def _():
                line_send[w, other] = kept[w, block_rows(other)].astype(bf16)
                combo_copy(w, other).start()

        line_send[w, buddy] = kept[w, block_rows(buddy)].astype(bf16)
        line_copy(w, buddy, couple, buddy).start()

    def pass_on(w):
        @pl.loop(0, chips)
        def _(step):
            other = far_first(z, chips, step)

            @pl.when(beyond_self(other))
            def _():
                combo_copy(w, other).wait_recv()
                total = kept[w, block_rows(other)] + combo[w, other].astype(f32)
                line_send[w, other] = total.astype(bf16)
                line_copy(w, other, couple, other).start()

    for s in range(slots):
        a_copy(s).wait()
    for n, w in enumerate(ORDER):
        take_stream(w)
        if n < 2:
            products(w, 0, own)
        else:
            pass_on(ORDER[0])
            give(ORDER[1])
            products(w, 0, own // 2)
            pass_on(ORDER[1])
            products(w, own // 2, own)
        pair_send[w] = restrict(1 - k)
        pair_copy(w).start()
        kept[w] = restrict(k)
        if n == 1:
            give(ORDER[0])
    give(ORDER[2])
    pass_on(ORDER[2])

    for w in ORDER:
        columns = slice(w * wide, (w + 1) * wide)

        @pl.loop(0, chips // 2)
        def _(source):
            line_copy(w, buddy, source, buddy).wait_recv()
            out_ref[:, columns] += line_recv[w, source].astype(f32)

        @pl.loop(1, chips)
        def _(step):
            line_copy(w, (z + step) % chips, couple, buddy).wait_send()

        pair_copy(w).wait_send()

        @pl.loop(0, col_count)
        def _(other):
            slot = other * 3 + w

            @pl.when(group_ok(g + 1 - w) & ((other != c) | (w != 1)))
            def _():
                cols_copy(slot, slot, g + 1 - w, other).wait_send()
                tiles_copy(slot, slot, g + 1 - w, other).wait_send()


def body(row_count, col_count, a_tiles, a_cols, p_tiles, p_cols, send_list):
    own, slots = a_cols.shape
    tiles = p_cols.shape[1]
    bs = a_tiles.shape[-1]
    ghosts = 3 * col_count
    chips = col_count // 2
    wide = CG * bs
    piece = wide // col_count
    vmem = pl.BlockSpec(memory_space=pltpu.VMEM)
    smem = pl.BlockSpec(memory_space=pltpu.SMEM)
    dma = pltpu.SemaphoreType.DMA
    f32, bf16 = jnp.float32, jnp.bfloat16
    return pl.pallas_call(
        functools.partial(kernel, row_count, col_count),
        out_shape=jax.ShapeDtypeStruct((piece, 3 * wide), f32),
        in_specs=[pl.BlockSpec(memory_space=pl.ANY), vmem, smem, smem, smem],
        out_specs=vmem,
        scratch_shapes=[
            pltpu.VMEM((own, bs, slots * bs), bf16),
            pltpu.VMEM((ghosts, tiles, bs, bs), bf16),
            pltpu.VMEM((ghosts, 1, tiles * bs), jnp.int32),
            pltpu.VMEM((ghosts, tiles, bs, bs), bf16),
            pltpu.VMEM((ghosts, 1, tiles * bs), jnp.int32),
            pltpu.VMEM((own + ghosts + 1, bs, wide), bf16),
            pltpu.VMEM((wide, own * bs), bf16),
            pltpu.VMEM((own * bs, wide), bf16),
            pltpu.VMEM((3, wide // 2, wide), f32),
            pltpu.VMEM((3, wide // 2, wide), f32),
            pltpu.VMEM((3, wide // 2, wide), f32),
            pltpu.VMEM((3, chips, piece, wide), bf16),
            pltpu.VMEM((3, chips, piece, wide), bf16),
            pltpu.VMEM((3, chips // 2, piece, wide), bf16),
            dma((slots,)),
            dma((ghosts,)), dma((ghosts,)), dma((ghosts,)), dma((ghosts,)),
            dma((3,)), dma((3,)), dma((3, chips)), dma((3, chips)), dma((3, chips // 2)),
        ],
        compiler_params=pltpu.CompilerParams(
            collective_id=0, has_side_effects=True, vmem_limit_bytes=VMEM_LIMIT
        ),
        name="triple_product",
    )(a_tiles, p_tiles, a_cols, p_cols.T, send_list)


def solution(mesh):
    in_specs = (
        P(("row", "col"), None, None, None),
        P(("row", "col"), None),
        P(("row", "col"), None, None, None),
        P(("row", "col"), None),
        P(("row", "col"), None),
    )
    out_specs = P(("row", "col"), None)
    return jax.shard_map(
        functools.partial(body, mesh.shape["row"], mesh.shape["col"]),
        mesh=mesh, in_specs=in_specs, out_specs=out_specs, check_vma=False,
    )
```

```python
import functools

import jax
import jax.numpy as jnp
from jax import lax
from jax.experimental import pallas as pl
from jax.experimental.pallas import tpu as pltpu
from jax.sharding import PartitionSpec as P

CG = 4
MESH = pl.DeviceIdType.MESH
ORDER = (1, 0, 2)
VMEM_LIMIT = 56 * 1024 * 1024


def far_first(index, count, step):
    half = count // 2
    side, local = index // half, index % half
    side = jnp.where(step < half, 1 - side, side)
    return side * half + (local + step) % half


def kernel(
    row_count, col_count, a_hbm, p_ref, ac_ref, pc_ref, sl_ref, out_ref,
    a_vm, send, send_cols, recv, recv_cols, dense, rt, prod,
    pair_send, pair_recv, kept, line_send, combo, line_recv,
    a_sem, tile_ss, tile_rs, cols_ss, cols_rs, pair_ss, pair_rs, line_ss, combo_rs, line_rs,
):
    g, c = lax.axis_index("row"), lax.axis_index("col")
    chips = col_count // 2
    z, k = c // 2, c % 2
    own, slots = ac_ref.shape
    bs = p_ref.shape[-1]
    ghosts = 3 * col_count
    zero_row = own + ghosts
    wide = CG * bs
    piece = wide // col_count
    half = wide // 2
    couple = z // 2
    buddy = z + 1 - 2 * (z % 2)
    f32, bf16 = jnp.float32, jnp.bfloat16

    def group_ok(group):
        return (group >= 0) & (group < row_count)

    def a_copy(s):
        return pltpu.make_async_copy(
            a_hbm.at[:, s], a_vm.at[:, :, pl.ds(s * bs, bs)], a_sem.at[s]
        )

    barrier = pltpu.get_barrier_semaphore()

    @pl.loop(0, col_count)
    def _(other):
        for t in range(3):
            group = g + 1 - t

            @pl.when(group_ok(group) & ((other != c) | (t != 1)))
            def _():
                pl.semaphore_signal(barrier, inc=1, device_id=(group, other), device_id_type=MESH)

    for s in range(slots):
        a_copy(s).start()

    def pattern(r):
        lane = lax.broadcasted_iota(jnp.int32, (1, 2 * bs), 1)
        return jnp.where(lane < bs, pc_ref[0, r], pc_ref[1, r])

    @pl.loop(0, col_count)
    def _(other):
        for t in range(3):
            j = other * 3 + t
            r = sl_ref[0, j]
            send[j, 0] = p_ref[r, 0]
            send[j, 1] = p_ref[r, 1]
            send_cols[j] = pattern(r)

    peers = col_count - 1
    peers = peers + jnp.where(g > 0, col_count, 0) + jnp.where(g < row_count - 1, col_count, 0)
    pl.semaphore_wait(barrier, peers)

    def tiles_copy(source, target, group, other):
        return pltpu.make_async_remote_copy(
            src_ref=send.at[source], dst_ref=recv.at[target],
            send_sem=tile_ss.at[source], recv_sem=tile_rs.at[target],
            device_id=(group, other), device_id_type=MESH,
        )

    def cols_copy(source, target, group, other):
        return pltpu.make_async_remote_copy(
            src_ref=send_cols.at[source], dst_ref=recv_cols.at[target],
            send_sem=cols_ss.at[source], recv_sem=cols_rs.at[target],
            device_id=(group, other), device_id_type=MESH,
        )

    def pair_copy(w):
        return pltpu.make_async_remote_copy(
            src_ref=pair_send.at[w], dst_ref=pair_recv.at[w],
            send_sem=pair_ss.at[w], recv_sem=pair_rs.at[w],
            device_id=(g, 2 * z + 1 - k), device_id_type=MESH,
        )

    def line_copy(w, block, target, other):
        return pltpu.make_async_remote_copy(
            src_ref=line_send.at[w, block], dst_ref=line_recv.at[w, target],
            send_sem=line_ss.at[w, block], recv_sem=line_rs.at[w, target],
            device_id=(g, 2 * other + k), device_id_type=MESH,
        )

    def combo_copy(w, block):
        return pltpu.make_async_remote_copy(
            src_ref=line_send.at[w, block], dst_ref=combo.at[w, block],
            send_sem=line_ss.at[w, block], recv_sem=combo_rs.at[w, block],
            device_id=(g, 2 * buddy + k), device_id_type=MESH,
        )

    def start_stream(t):
        group = g + 1 - t

        @pl.loop(0, col_count)
        def _(step):
            other = far_first(c, col_count, step)

            @pl.when(group_ok(group) & ((other != c) | (t != 1)))
            def _():
                cols_copy(other * 3 + t, c * 3 + t, group, other).start()
                tiles_copy(other * 3 + t, c * 3 + t, group, other).start()

    def finish_stream(t):
        group = g + 1 - t

        @pl.loop(0, col_count)
        def _(other):
            slot = other * 3 + t

            @pl.when(group_ok(group) & ((other != c) | (t != 1)))
            def _():
                cols_copy(slot, slot, group, other).wait_send()
                tiles_copy(slot, slot, group, other).wait_send()

    start_stream(ORDER[0])
    start_stream(ORDER[1])

    def spread(target, tiles, cols):
        first, second = tiles[0].astype(f32), tiles[1].astype(f32)
        for m in range(CG):
            in_first = jnp.where(cols[:, :bs] == m, 1.0, 0.0)
            in_second = jnp.where(cols[:, bs:] == m, 1.0, 0.0)
            dense[target, :, m * bs : (m + 1) * bs] = (
                first * in_first + second * in_second
            ).astype(bf16)

    dense[zero_row] = jnp.zeros((bs, wide), bf16)
    owners = col_count // CG

    @pl.loop(0, own)
    def _(r):
        spread(r, p_ref.at[r], pattern(r))
        first = p_ref[r, 0].astype(f32).T
        second = p_ref[r, 1].astype(f32).T
        for m in range(CG):
            in_first = jnp.where(pc_ref[0, r] == m, 1.0, 0.0)
            in_second = jnp.where(pc_ref[1, r] == m, 1.0, 0.0)
            block = (first * in_first + second * in_second).astype(bf16)
            for u in range(owners):
                start = (u % 2) * half + (m * (owners // 2) + u // 2) * piece
                rt[start : start + piece, pl.ds(pl.multiple_of(r * bs, bs), bs)] = block[
                    u * piece : (u + 1) * piece
                ]

    def take_stream(t):
        @pl.loop(0, col_count)
        def _(other):
            slot = other * 3 + t

            @pl.when(group_ok(g + t - 1) & ((other != c) | (t != 1)))
            def _():
                cols_copy(slot, slot, g + t - 1, other).wait_recv()
                tiles_copy(slot, slot, g + t - 1, other).wait_recv()
                spread(own + slot, recv.at[slot], recv_cols[slot])

            if t == 1:

                @pl.when(other == c)
                def _():
                    spread(own + slot, send.at[slot], send_cols[slot])

    def products(w, low, high):
        @pl.loop(low, high)
        def _(i):
            index = []
            for s in range(slots):
                b = ac_ref[i, s]
                ghost = jnp.maximum(b - own, 0)
                stream = jnp.where(b < own, 1, ghost % 3)
                index.append(jnp.where((b >= 0) & (stream == w), b, zero_row))
            for n in range(0, wide, 2 * bs):
                total = jnp.zeros((bs, 2 * bs), f32)
                for s in range(0, slots, 2):
                    right = jnp.concatenate(
                        [dense[index[s], :, n : n + 2 * bs], dense[index[s + 1], :, n : n + 2 * bs]],
                        axis=0,
                    )
                    left = a_vm[i, :, s * bs : (s + 2) * bs]
                    total = total + jnp.dot(left, right, preferred_element_type=f32)
                prod[pl.ds(pl.multiple_of(i * bs, bs), bs), n : n + 2 * bs] = total.astype(bf16)

    def restrict(core):
        rows = rt[pl.ds(pl.multiple_of(core * half, half), half), :]
        return jnp.dot(rows, prod[...], preferred_element_type=f32)

    def block_rows(other):
        return pl.ds(pl.multiple_of(other * piece, piece), piece)

    def beyond_buddy(other):
        return jnp.where(z % 2 == 0, other > z + 1, other < z - 1)

    def beyond_self(other):
        return jnp.where(z % 2 == 0, other < z, other > z)

    def give(w):
        pair_copy(w).wait_recv()
        kept[w] = kept[w] + pair_recv[w]
        out_ref[:, w * wide : (w + 1) * wide] = kept[w, block_rows(z)]

        @pl.loop(0, chips)
        def _(step):
            other = far_first(z, chips, step)

            @pl.when(beyond_buddy(other))
            def _():
                line_send[w, other] = kept[w, block_rows(other)].astype(bf16)
                combo_copy(w, other).start()

        line_send[w, buddy] = kept[w, block_rows(buddy)].astype(bf16)
        line_copy(w, buddy, couple, buddy).start()

    def pass_on(w):
        @pl.loop(0, chips)
        def _(step):
            other = far_first(z, chips, step)

            @pl.when(beyond_self(other))
            def _():
                combo_copy(w, other).wait_recv()
                total = kept[w, block_rows(other)] + combo[w, other].astype(f32)
                line_send[w, other] = total.astype(bf16)
                line_copy(w, other, couple, other).start()

    for s in range(slots):
        a_copy(s).wait()
    for n, w in enumerate(ORDER):
        take_stream(w)
        finish_stream(w)
        if n == 0:
            start_stream(ORDER[2])
        if n < 2:
            products(w, 0, own)
        else:
            pass_on(ORDER[0])
            give(ORDER[1])
            products(w, 0, own // 2)
            pass_on(ORDER[1])
            products(w, own // 2, own)
        pair_send[w] = restrict(1 - k)
        pair_copy(w).start()
        kept[w] = restrict(k)
        if n == 1:
            give(ORDER[0])
    give(ORDER[2])
    pass_on(ORDER[2])

    for w in ORDER:
        columns = slice(w * wide, (w + 1) * wide)

        @pl.loop(0, chips // 2)
        def _(source):
            line_copy(w, buddy, source, buddy).wait_recv()
            out_ref[:, columns] += line_recv[w, source].astype(f32)

        @pl.loop(1, chips)
        def _(step):
            line_copy(w, (z + step) % chips, couple, buddy).wait_send()

        pair_copy(w).wait_send()


def body(row_count, col_count, a_tiles, a_cols, p_tiles, p_cols, send_list):
    own, slots = a_cols.shape
    tiles = p_cols.shape[1]
    bs = a_tiles.shape[-1]
    ghosts = 3 * col_count
    chips = col_count // 2
    wide = CG * bs
    piece = wide // col_count
    vmem = pl.BlockSpec(memory_space=pltpu.VMEM)
    smem = pl.BlockSpec(memory_space=pltpu.SMEM)
    dma = pltpu.SemaphoreType.DMA
    f32, bf16 = jnp.float32, jnp.bfloat16
    return pl.pallas_call(
        functools.partial(kernel, row_count, col_count),
        out_shape=jax.ShapeDtypeStruct((piece, 3 * wide), f32),
        in_specs=[pl.BlockSpec(memory_space=pl.ANY), vmem, smem, smem, smem],
        out_specs=vmem,
        scratch_shapes=[
            pltpu.VMEM((own, bs, slots * bs), bf16),
            pltpu.VMEM((ghosts, tiles, bs, bs), bf16),
            pltpu.VMEM((ghosts, 1, tiles * bs), jnp.int32),
            pltpu.VMEM((ghosts, tiles, bs, bs), bf16),
            pltpu.VMEM((ghosts, 1, tiles * bs), jnp.int32),
            pltpu.VMEM((own + ghosts + 1, bs, wide), bf16),
            pltpu.VMEM((wide, own * bs), bf16),
            pltpu.VMEM((own * bs, wide), bf16),
            pltpu.VMEM((3, wide // 2, wide), f32),
            pltpu.VMEM((3, wide // 2, wide), f32),
            pltpu.VMEM((3, wide // 2, wide), f32),
            pltpu.VMEM((3, chips, piece, wide), bf16),
            pltpu.VMEM((3, chips, piece, wide), bf16),
            pltpu.VMEM((3, chips // 2, piece, wide), bf16),
            dma((slots,)),
            dma((ghosts,)), dma((ghosts,)), dma((ghosts,)), dma((ghosts,)),
            dma((3,)), dma((3,)), dma((3, chips)), dma((3, chips)), dma((3, chips // 2)),
        ],
        compiler_params=pltpu.CompilerParams(
            collective_id=0, has_side_effects=True, vmem_limit_bytes=VMEM_LIMIT
        ),
        name="triple_product",
    )(a_tiles, p_tiles, a_cols, p_cols.T, send_list)


def solution(mesh):
    in_specs = (
        P(("row", "col"), None, None, None),
        P(("row", "col"), None),
        P(("row", "col"), None, None, None),
        P(("row", "col"), None),
        P(("row", "col"), None),
    )
    out_specs = P(("row", "col"), None)
    return jax.shard_map(
        functools.partial(body, mesh.shape["row"], mesh.shape["col"]),
        mesh=mesh, in_specs=in_specs, out_specs=out_specs, check_vma=False,
    )
```

```python
import functools

import jax
import jax.numpy as jnp
from jax import lax
from jax.experimental import pallas as pl
from jax.experimental.pallas import tpu as pltpu
from jax.sharding import PartitionSpec as P

CG = 4
MESH = pl.DeviceIdType.MESH
ORDER = (1, 0, 2)
VMEM_LIMIT = 56 * 1024 * 1024


def far_first(index, count, step):
    half = count // 2
    side, local = index // half, index % half
    side = jnp.where(step < half, 1 - side, side)
    return side * half + (local + step) % half


def kernel(
    row_count, col_count, a_hbm, p_ref, ac_ref, pc_ref, sl_ref, out_ref,
    a_vm, chain, a_first, a_other, following, send, send_cols, recv, recv_cols, dense, rt, prod,
    pair_send, pair_recv, kept, line_send, combo, line_recv,
    a_sem, tile_ss, tile_rs, cols_ss, cols_rs, pair_ss, pair_rs, line_ss, combo_rs, line_rs,
):
    g, c = lax.axis_index("row"), lax.axis_index("col")
    chips = col_count // 2
    z, k = c // 2, c % 2
    own, slots = ac_ref.shape
    bs = p_ref.shape[-1]
    ghosts = 3 * col_count
    wide = CG * bs
    piece = wide // col_count
    half = wide // 2
    couple = z // 2
    buddy = z + 1 - 2 * (z % 2)
    f32, bf16 = jnp.float32, jnp.bfloat16

    def group_ok(group):
        return (group >= 0) & (group < row_count)

    a_copy = pltpu.make_async_copy(a_hbm, a_vm, a_sem)
    barrier = pltpu.get_barrier_semaphore()

    @pl.loop(0, col_count)
    def _(other):
        for t in range(3):
            group = g + 1 - t

            @pl.when(group_ok(group) & ((other != c) | (t != 1)))
            def _():
                pl.semaphore_signal(barrier, inc=1, device_id=(group, other), device_id_type=MESH)

    a_copy.start()

    def pattern(r):
        lane = lax.broadcasted_iota(jnp.int32, (1, 2 * bs), 1)
        return jnp.where(lane < bs, pc_ref[0, r], pc_ref[1, r])

    @pl.loop(0, col_count)
    def _(other):
        for t in range(3):
            j = other * 3 + t
            r = sl_ref[0, j]
            send[j, 0] = p_ref[r, 0]
            send[j, 1] = p_ref[r, 1]
            send_cols[j] = pattern(r)

    peers = col_count - 1
    peers = peers + jnp.where(g > 0, col_count, 0) + jnp.where(g < row_count - 1, col_count, 0)
    pl.semaphore_wait(barrier, peers)

    def tiles_copy(source, target, group, other):
        return pltpu.make_async_remote_copy(
            src_ref=send.at[source], dst_ref=recv.at[target],
            send_sem=tile_ss.at[source], recv_sem=tile_rs.at[target],
            device_id=(group, other), device_id_type=MESH,
        )

    def cols_copy(source, target, group, other):
        return pltpu.make_async_remote_copy(
            src_ref=send_cols.at[source], dst_ref=recv_cols.at[target],
            send_sem=cols_ss.at[source], recv_sem=cols_rs.at[target],
            device_id=(group, other), device_id_type=MESH,
        )

    def pair_copy(w):
        return pltpu.make_async_remote_copy(
            src_ref=pair_send.at[w], dst_ref=pair_recv.at[w],
            send_sem=pair_ss.at[w], recv_sem=pair_rs.at[w],
            device_id=(g, 2 * z + 1 - k), device_id_type=MESH,
        )

    def line_copy(w, block, target, other):
        return pltpu.make_async_remote_copy(
            src_ref=line_send.at[w, block], dst_ref=line_recv.at[w, target],
            send_sem=line_ss.at[w, block], recv_sem=line_rs.at[w, target],
            device_id=(g, 2 * other + k), device_id_type=MESH,
        )

    def combo_copy(w, block):
        return pltpu.make_async_remote_copy(
            src_ref=line_send.at[w, block], dst_ref=combo.at[w, block],
            send_sem=line_ss.at[w, block], recv_sem=combo_rs.at[w, block],
            device_id=(g, 2 * buddy + k), device_id_type=MESH,
        )

    def start_stream(t):
        group = g + 1 - t

        @pl.loop(0, col_count)
        def _(step):
            other = far_first(c, col_count, step)

            @pl.when(group_ok(group) & ((other != c) | (t != 1)))
            def _():
                cols_copy(other * 3 + t, c * 3 + t, group, other).start()
                tiles_copy(other * 3 + t, c * 3 + t, group, other).start()

    def finish_stream(t):
        group = g + 1 - t

        @pl.loop(0, col_count)
        def _(other):
            slot = other * 3 + t

            @pl.when(group_ok(group) & ((other != c) | (t != 1)))
            def _():
                cols_copy(slot, slot, group, other).wait_send()
                tiles_copy(slot, slot, group, other).wait_send()

    for t in ORDER:
        start_stream(t)

    def spread(target, tiles, cols):
        first, second = tiles[0].astype(f32), tiles[1].astype(f32)
        for m in range(CG):
            in_first = jnp.where(cols[:, :bs] == m, 1.0, 0.0)
            in_second = jnp.where(cols[:, bs:] == m, 1.0, 0.0)
            dense[pl.ds(pl.multiple_of(target * bs, bs), bs), m * bs : (m + 1) * bs] = (
                first * in_first + second * in_second
            ).astype(bf16)

    owners = col_count // CG

    @pl.loop(0, own)
    def _(r):
        spread(col_count + r, p_ref.at[r], pattern(r))
        first = p_ref[r, 0].astype(f32).T
        second = p_ref[r, 1].astype(f32).T
        for m in range(CG):
            in_first = jnp.where(pc_ref[0, r] == m, 1.0, 0.0)
            in_second = jnp.where(pc_ref[1, r] == m, 1.0, 0.0)
            block = (first * in_first + second * in_second).astype(bf16)
            for u in range(owners):
                start = (u % 2) * half + (m * (owners // 2) + u // 2) * piece
                rt[start : start + piece, pl.ds(pl.multiple_of(r * bs, bs), bs)] = block[
                    u * piece : (u + 1) * piece
                ]

    def take_stream(t):
        @pl.loop(0, col_count)
        def _(other):
            slot = other * 3 + t

            @pl.when(group_ok(g + t - 1) & ((other != c) | (t != 1)))
            def _():
                cols_copy(slot, slot, g + t - 1, other).wait_recv()
                tiles_copy(slot, slot, g + t - 1, other).wait_recv()
                spread(other, recv.at[slot], recv_cols[slot])

            if t == 1:

                @pl.when(other == c)
                def _():
                    spread(other, send.at[slot], send_cols[slot])

    @pl.loop(0, own)
    def _(i):
        for s in range(slots):
            after = jnp.int32(slots)
            for later in range(slots - 1, s, -1):
                after = jnp.where(ac_ref[i, later] == ac_ref[i, s], later, after)
            following[i, s] = after

    chain[slots] = jnp.zeros((bs, bs), f32)

    def lay_out(parts):
        @pl.loop(0, own)
        def _(i):
            for s in range(slots - 1, -1, -1):
                chain[s] = a_vm[i, s].astype(f32) + chain[following[i, s]]
            rows = pl.ds(pl.multiple_of(i * bs, bs), bs)

            def place(target, position, b):
                first = jnp.int32(slots)
                for s in range(slots - 1, -1, -1):
                    first = jnp.where(ac_ref[i, s] == b, s, first)
                columns = pl.ds(pl.multiple_of(position * bs, bs), bs)
                target[rows, columns] = chain[first].astype(bf16)

            for t, target in parts:

                @pl.loop(0, col_count)
                def _(q):
                    place(target, q, own + 3 * q + t)

                if t == 1:

                    @pl.loop(0, own)
                    def _(r):
                        place(target, col_count + r, r)

    def products(a_part, depth, low, high):
        step_rows = 2 * bs

        @pl.loop(low, high)
        def _(step):
            rows = pl.ds(pl.multiple_of(step * step_rows, step_rows), step_rows)
            prod[rows, :] = jnp.dot(
                a_part[rows, :depth], dense[:depth, :], preferred_element_type=f32
            ).astype(bf16)

    def restrict(core):
        rows = rt[pl.ds(pl.multiple_of(core * half, half), half), :]
        return jnp.dot(rows, prod[...], preferred_element_type=f32)

    def block_rows(other):
        return pl.ds(pl.multiple_of(other * piece, piece), piece)

    def beyond_buddy(other):
        return jnp.where(z % 2 == 0, other > z + 1, other < z - 1)

    def beyond_self(other):
        return jnp.where(z % 2 == 0, other < z, other > z)

    def give(w):
        pair_copy(w).wait_recv()
        kept[w] = kept[w] + pair_recv[w]
        out_ref[:, w * wide : (w + 1) * wide] = kept[w, block_rows(z)]

        @pl.loop(0, chips)
        def _(step):
            other = far_first(z, chips, step)

            @pl.when(beyond_buddy(other))
            def _():
                line_send[w, other] = kept[w, block_rows(other)].astype(bf16)
                combo_copy(w, other).start()

        line_send[w, buddy] = kept[w, block_rows(buddy)].astype(bf16)
        line_copy(w, buddy, couple, buddy).start()

    def pass_on(w):
        @pl.loop(0, chips)
        def _(step):
            other = far_first(z, chips, step)

            @pl.when(beyond_self(other))
            def _():
                combo_copy(w, other).wait_recv()
                total = kept[w, block_rows(other)] + combo[w, other].astype(f32)
                line_send[w, other] = total.astype(bf16)
                line_copy(w, other, couple, other).start()

    a_copy.wait()
    lay_out(((1, a_first), (0, a_other)))
    steps = own // 2
    ghost_depth = col_count * bs
    for n, w in enumerate(ORDER):
        take_stream(w)
        if n == 0:
            products(a_first, ghost_depth + own * bs, 0, steps)
        elif n == 1:
            products(a_other, ghost_depth, 0, steps)
        else:
            pass_on(ORDER[0])
            give(ORDER[1])
            products(a_first, ghost_depth, 0, steps // 2)
            pass_on(ORDER[1])
            products(a_first, ghost_depth, steps // 2, steps)
        pair_send[w] = restrict(1 - k)
        pair_copy(w).start()
        kept[w] = restrict(k)
        if n == 0:
            lay_out(((2, a_first),))
        if n == 1:
            give(ORDER[0])
    give(ORDER[2])
    pass_on(ORDER[2])

    for w in ORDER:
        columns = slice(w * wide, (w + 1) * wide)

        @pl.loop(0, chips // 2)
        def _(source):
            line_copy(w, buddy, source, buddy).wait_recv()
            out_ref[:, columns] += line_recv[w, source].astype(f32)

        @pl.loop(1, chips)
        def _(step):
            line_copy(w, (z + step) % chips, couple, buddy).wait_send()

        pair_copy(w).wait_send()
        finish_stream(w)


def body(row_count, col_count, a_tiles, a_cols, p_tiles, p_cols, send_list):
    own, slots = a_cols.shape
    tiles = p_cols.shape[1]
    bs = a_tiles.shape[-1]
    ghosts = 3 * col_count
    chips = col_count // 2
    wide = CG * bs
    piece = wide // col_count
    vmem = pl.BlockSpec(memory_space=pltpu.VMEM)
    smem = pl.BlockSpec(memory_space=pltpu.SMEM)
    dma = pltpu.SemaphoreType.DMA
    f32, bf16 = jnp.float32, jnp.bfloat16
    return pl.pallas_call(
        functools.partial(kernel, row_count, col_count),
        out_shape=jax.ShapeDtypeStruct((piece, 3 * wide), f32),
        in_specs=[pl.BlockSpec(memory_space=pl.ANY), vmem, smem, smem, smem],
        out_specs=vmem,
        scratch_shapes=[
            pltpu.VMEM((own, slots, bs, bs), bf16),
            pltpu.VMEM((slots + 1, bs, bs), f32),
            pltpu.VMEM((own * bs, (col_count + own) * bs), bf16),
            pltpu.VMEM((own * bs, col_count * bs), bf16),
            pltpu.SMEM((own, slots), jnp.int32),
            pltpu.VMEM((ghosts, tiles, bs, bs), bf16),
            pltpu.VMEM((ghosts, 1, tiles * bs), jnp.int32),
            pltpu.VMEM((ghosts, tiles, bs, bs), bf16),
            pltpu.VMEM((ghosts, 1, tiles * bs), jnp.int32),
            pltpu.VMEM(((col_count + own) * bs, wide), bf16),
            pltpu.VMEM((wide, own * bs), bf16),
            pltpu.VMEM((own * bs, wide), bf16),
            pltpu.VMEM((3, wide // 2, wide), f32),
            pltpu.VMEM((3, wide // 2, wide), f32),
            pltpu.VMEM((3, wide // 2, wide), f32),
            pltpu.VMEM((3, chips, piece, wide), bf16),
            pltpu.VMEM((3, chips, piece, wide), bf16),
            pltpu.VMEM((3, chips // 2, piece, wide), bf16),
            dma,
            dma((ghosts,)), dma((ghosts,)), dma((ghosts,)), dma((ghosts,)),
            dma((3,)), dma((3,)), dma((3, chips)), dma((3, chips)), dma((3, chips // 2)),
        ],
        compiler_params=pltpu.CompilerParams(
            collective_id=0, has_side_effects=True, vmem_limit_bytes=VMEM_LIMIT
        ),
        name="triple_product",
    )(a_tiles, p_tiles, a_cols, p_cols.T, send_list)


def solution(mesh):
    in_specs = (
        P(("row", "col"), None, None, None),
        P(("row", "col"), None),
        P(("row", "col"), None, None, None),
        P(("row", "col"), None),
        P(("row", "col"), None),
    )
    out_specs = P(("row", "col"), None)
    return jax.shard_map(
        functools.partial(body, mesh.shape["row"], mesh.shape["col"]),
        mesh=mesh, in_specs=in_specs, out_specs=out_specs, check_vma=False,
    )
```

```python
import functools

import jax
import jax.numpy as jnp
from jax import lax
from jax.experimental import pallas as pl
from jax.experimental.pallas import tpu as pltpu
from jax.sharding import PartitionSpec as P

CG = 4
MESH = pl.DeviceIdType.MESH
ORDER = (1, 0, 2)
VMEM_LIMIT = 56 * 1024 * 1024


def far_first(index, count, step):
    half = count // 2
    side, local = index // half, index % half
    side = jnp.where(step < half, 1 - side, side)
    return side * half + (local + step) % half


def kernel(
    row_count, col_count, a_hbm, p_ref, ac_ref, pc_ref, sl_ref, out_ref,
    a_vm, chain, a_high, a_low, following, send, send_cols, recv, recv_cols, dense, rt, prod,
    pair_send, pair_recv, kept, line_send, combo, line_recv,
    a_sem, tile_ss, tile_rs, cols_ss, cols_rs, pair_ss, pair_rs, line_ss, combo_rs, line_rs,
):
    g, c = lax.axis_index("row"), lax.axis_index("col")
    chips = col_count // 2
    z, k = c // 2, c % 2
    own, slots = ac_ref.shape
    bs = p_ref.shape[-1]
    ghosts = 3 * col_count
    wide = CG * bs
    piece = wide // col_count
    half = wide // 2
    couple = z // 2
    buddy = z + 1 - 2 * (z % 2)
    f32, bf16 = jnp.float32, jnp.bfloat16

    def group_ok(group):
        return (group >= 0) & (group < row_count)

    a_copy = pltpu.make_async_copy(a_hbm, a_vm, a_sem)
    barrier = pltpu.get_barrier_semaphore()

    @pl.loop(0, col_count)
    def _(other):
        for t in range(3):
            group = g + 1 - t

            @pl.when(group_ok(group) & ((other != c) | (t != 1)))
            def _():
                pl.semaphore_signal(barrier, inc=1, device_id=(group, other), device_id_type=MESH)

    a_copy.start()

    def pattern(r):
        lane = lax.broadcasted_iota(jnp.int32, (1, 2 * bs), 1)
        return jnp.where(lane < bs, pc_ref[0, r], pc_ref[1, r])

    @pl.loop(0, col_count)
    def _(other):
        for t in range(3):
            j = other * 3 + t
            r = sl_ref[0, j]
            send[j, 0] = p_ref[r, 0]
            send[j, 1] = p_ref[r, 1]
            send_cols[j] = pattern(r)

    peers = col_count - 1
    peers = peers + jnp.where(g > 0, col_count, 0) + jnp.where(g < row_count - 1, col_count, 0)
    pl.semaphore_wait(barrier, peers)

    def tiles_copy(source, target, group, other):
        return pltpu.make_async_remote_copy(
            src_ref=send.at[source], dst_ref=recv.at[target],
            send_sem=tile_ss.at[source], recv_sem=tile_rs.at[target],
            device_id=(group, other), device_id_type=MESH,
        )

    def cols_copy(source, target, group, other):
        return pltpu.make_async_remote_copy(
            src_ref=send_cols.at[source], dst_ref=recv_cols.at[target],
            send_sem=cols_ss.at[source], recv_sem=cols_rs.at[target],
            device_id=(group, other), device_id_type=MESH,
        )

    def pair_copy(w):
        return pltpu.make_async_remote_copy(
            src_ref=pair_send.at[w], dst_ref=pair_recv.at[w],
            send_sem=pair_ss.at[w], recv_sem=pair_rs.at[w],
            device_id=(g, 2 * z + 1 - k), device_id_type=MESH,
        )

    def line_copy(w, block, target, other):
        return pltpu.make_async_remote_copy(
            src_ref=line_send.at[w, block], dst_ref=line_recv.at[w, target],
            send_sem=line_ss.at[w, block], recv_sem=line_rs.at[w, target],
            device_id=(g, 2 * other + k), device_id_type=MESH,
        )

    def combo_copy(w, block):
        return pltpu.make_async_remote_copy(
            src_ref=line_send.at[w, block], dst_ref=combo.at[w, block],
            send_sem=line_ss.at[w, block], recv_sem=combo_rs.at[w, block],
            device_id=(g, 2 * buddy + k), device_id_type=MESH,
        )

    def start_stream(t):
        group = g + 1 - t

        @pl.loop(0, col_count)
        def _(step):
            other = far_first(c, col_count, step)

            @pl.when(group_ok(group) & ((other != c) | (t != 1)))
            def _():
                cols_copy(other * 3 + t, c * 3 + t, group, other).start()
                tiles_copy(other * 3 + t, c * 3 + t, group, other).start()

    def finish_stream(t):
        group = g + 1 - t

        @pl.loop(0, col_count)
        def _(other):
            slot = other * 3 + t

            @pl.when(group_ok(group) & ((other != c) | (t != 1)))
            def _():
                cols_copy(slot, slot, group, other).wait_send()
                tiles_copy(slot, slot, group, other).wait_send()

    start_stream(ORDER[0])
    start_stream(ORDER[1])

    def spread(target, tiles, cols):
        first, second = tiles[0].astype(f32), tiles[1].astype(f32)
        for m in range(CG):
            in_first = jnp.where(cols[:, :bs] == m, 1.0, 0.0)
            in_second = jnp.where(cols[:, bs:] == m, 1.0, 0.0)
            dense[pl.ds(pl.multiple_of(target * bs, bs), bs), m * bs : (m + 1) * bs] = (
                first * in_first + second * in_second
            ).astype(bf16)

    owners = col_count // CG

    @pl.loop(0, own)
    def _(r):
        spread(col_count + r, p_ref.at[r], pattern(r))
        first = p_ref[r, 0].astype(f32).T
        second = p_ref[r, 1].astype(f32).T
        for m in range(CG):
            in_first = jnp.where(pc_ref[0, r] == m, 1.0, 0.0)
            in_second = jnp.where(pc_ref[1, r] == m, 1.0, 0.0)
            block = (first * in_first + second * in_second).astype(bf16)
            for u in range(owners):
                start = (u % 2) * half + (m * (owners // 2) + u // 2) * piece
                rt[start : start + piece, pl.ds(pl.multiple_of(r * bs, bs), bs)] = block[
                    u * piece : (u + 1) * piece
                ]

    def take_stream(t):
        @pl.loop(0, col_count)
        def _(other):
            slot = other * 3 + t

            @pl.when(group_ok(g + t - 1) & ((other != c) | (t != 1)))
            def _():
                cols_copy(slot, slot, g + t - 1, other).wait_recv()
                tiles_copy(slot, slot, g + t - 1, other).wait_recv()
                spread(other, recv.at[slot], recv_cols[slot])

            if t == 1:

                @pl.when(other == c)
                def _():
                    spread(other, send.at[slot], send_cols[slot])

    @pl.loop(0, own)
    def _(i):
        for s in range(slots):
            after = jnp.int32(slots)
            for later in range(slots - 1, s, -1):
                after = jnp.where(ac_ref[i, later] == ac_ref[i, s], later, after)
            following[i, s] = after

    chain[slots] = jnp.zeros((bs, bs), f32)

    def lay_out(t):
        @pl.loop(0, own)
        def _(i):
            for s in range(slots - 1, -1, -1):
                chain[s] = a_vm[i, s].astype(f32) + chain[following[i, s]]
            rows = pl.ds(pl.multiple_of(i * bs, bs), bs)

            def place(position, b):
                first = jnp.int32(slots)
                for s in range(slots - 1, -1, -1):
                    first = jnp.where(ac_ref[i, s] == b, s, first)
                columns = pl.ds(pl.multiple_of(position * bs, bs), bs)
                total = chain[first]
                high = total.astype(bf16)
                a_high[rows, columns] = high
                a_low[rows, columns] = (total - high.astype(f32)).astype(bf16)

            @pl.loop(0, col_count)
            def _(q):
                place(q, own + 3 * q + t)

            if t == 1:

                @pl.loop(0, own)
                def _(r):
                    place(col_count + r, r)

    def products(w):
        step_rows = 2 * bs
        depth = (col_count + (own if w == 1 else 0)) * bs

        @pl.loop(0, own // 2)
        def _(step):
            rows = pl.ds(pl.multiple_of(step * step_rows, step_rows), step_rows)
            right = dense[:depth, :]
            total = jnp.dot(a_high[rows, :depth], right, preferred_element_type=f32)
            total = total + jnp.dot(a_low[rows, :depth], right, preferred_element_type=f32)
            prod[rows, :] = total.astype(bf16)

    def restrict(core):
        rows = rt[pl.ds(pl.multiple_of(core * half, half), half), :]
        return jnp.dot(rows, prod[...], preferred_element_type=f32)

    def block_rows(other):
        return pl.ds(pl.multiple_of(other * piece, piece), piece)

    def beyond_buddy(other):
        return jnp.where(z % 2 == 0, other > z + 1, other < z - 1)

    def beyond_self(other):
        return jnp.where(z % 2 == 0, other < z, other > z)

    def give(w):
        pair_copy(w).wait_recv()
        kept[w] = kept[w] + pair_recv[w]
        out_ref[:, w * wide : (w + 1) * wide] = kept[w, block_rows(z)]

        @pl.loop(0, chips)
        def _(step):
            other = far_first(z, chips, step)

            @pl.when(beyond_buddy(other))
            def _():
                line_send[w, other] = kept[w, block_rows(other)].astype(bf16)
                combo_copy(w, other).start()

        line_send[w, buddy] = kept[w, block_rows(buddy)].astype(bf16)
        line_copy(w, buddy, couple, buddy).start()

    def give_straight(w):
        pair_copy(w).wait_recv()

        @pl.loop(0, chips)
        def _(step):
            other = far_first(z, chips, step)

            @pl.when(other != z)
            def _():
                total = kept[w, block_rows(other)] + pair_recv[w, block_rows(other)]
                line_send[w, other] = total.astype(bf16)
                line_copy(w, other, z, other).start()

        out_ref[:, w * wide : (w + 1) * wide] = (
            kept[w, block_rows(z)] + pair_recv[w, block_rows(z)]
        )

    def pass_on(w):
        @pl.loop(0, chips)
        def _(step):
            other = far_first(z, chips, step)

            @pl.when(beyond_self(other))
            def _():
                combo_copy(w, other).wait_recv()
                total = kept[w, block_rows(other)] + combo[w, other].astype(f32)
                line_send[w, other] = total.astype(bf16)
                line_copy(w, other, couple, other).start()

    a_copy.wait()
    lay_out(ORDER[0])
    for n, w in enumerate(ORDER):
        take_stream(w)
        if n == 0:
            finish_stream(w)
            start_stream(ORDER[2])
        products(w)
        pair_send[w] = restrict(1 - k)
        pair_copy(w).start()
        kept[w] = restrict(k)
        if n < 2:
            lay_out(ORDER[n + 1])
        if n == 1:
            give(ORDER[0])
            pass_on(ORDER[0])
            give(ORDER[1])
            pass_on(ORDER[1])
    give_straight(ORDER[2])

    for n, w in enumerate(ORDER):
        columns = slice(w * wide, (w + 1) * wide)

        @pl.loop(0, chips // 2 if n < 2 else chips - 1)
        def _(step):
            source = step if n < 2 else (z + 1 + step) % chips
            line_copy(w, buddy, source, buddy).wait_recv()
            out_ref[:, columns] += line_recv[w, source].astype(f32)

        @pl.loop(1, chips)
        def _(step):
            line_copy(w, (z + step) % chips, couple, buddy).wait_send()

        if n > 0:
            finish_stream(w)
        pair_copy(w).wait_send()


def body(row_count, col_count, a_tiles, a_cols, p_tiles, p_cols, send_list):
    own, slots = a_cols.shape
    tiles = p_cols.shape[1]
    bs = a_tiles.shape[-1]
    ghosts = 3 * col_count
    chips = col_count // 2
    wide = CG * bs
    piece = wide // col_count
    vmem = pl.BlockSpec(memory_space=pltpu.VMEM)
    smem = pl.BlockSpec(memory_space=pltpu.SMEM)
    dma = pltpu.SemaphoreType.DMA
    f32, bf16 = jnp.float32, jnp.bfloat16
    return pl.pallas_call(
        functools.partial(kernel, row_count, col_count),
        out_shape=jax.ShapeDtypeStruct((piece, 3 * wide), f32),
        in_specs=[pl.BlockSpec(memory_space=pl.ANY), vmem, smem, smem, smem],
        out_specs=vmem,
        scratch_shapes=[
            pltpu.VMEM((own, slots, bs, bs), bf16),
            pltpu.VMEM((slots + 1, bs, bs), f32),
            pltpu.VMEM((own * bs, (col_count + own) * bs), bf16),
            pltpu.VMEM((own * bs, (col_count + own) * bs), bf16),
            pltpu.SMEM((own, slots), jnp.int32),
            pltpu.VMEM((ghosts, tiles, bs, bs), bf16),
            pltpu.VMEM((ghosts, 1, tiles * bs), jnp.int32),
            pltpu.VMEM((ghosts, tiles, bs, bs), bf16),
            pltpu.VMEM((ghosts, 1, tiles * bs), jnp.int32),
            pltpu.VMEM(((col_count + own) * bs, wide), bf16),
            pltpu.VMEM((wide, own * bs), bf16),
            pltpu.VMEM((own * bs, wide), bf16),
            pltpu.VMEM((3, wide // 2, wide), f32),
            pltpu.VMEM((3, wide // 2, wide), f32),
            pltpu.VMEM((3, wide // 2, wide), f32),
            pltpu.VMEM((3, chips, piece, wide), bf16),
            pltpu.VMEM((3, chips, piece, wide), bf16),
            pltpu.VMEM((3, chips, piece, wide), bf16),
            dma,
            dma((ghosts,)), dma((ghosts,)), dma((ghosts,)), dma((ghosts,)),
            dma((3,)), dma((3,)), dma((3, chips)), dma((3, chips)), dma((3, chips)),
        ],
        compiler_params=pltpu.CompilerParams(
            collective_id=0, has_side_effects=True, vmem_limit_bytes=VMEM_LIMIT
        ),
        name="triple_product",
    )(a_tiles, p_tiles, a_cols, p_cols.T, send_list)


def solution(mesh):
    in_specs = (
        P(("row", "col"), None, None, None),
        P(("row", "col"), None),
        P(("row", "col"), None, None, None),
        P(("row", "col"), None),
        P(("row", "col"), None),
    )
    out_specs = P(("row", "col"), None)
    return jax.shard_map(
        functools.partial(body, mesh.shape["row"], mesh.shape["col"]),
        mesh=mesh, in_specs=in_specs, out_specs=out_specs, check_vma=False,
    )
```

```python
import functools

import jax
import jax.numpy as jnp
from jax import lax
from jax.experimental import pallas as pl
from jax.experimental.pallas import tpu as pltpu
from jax.sharding import PartitionSpec as P

CG = 4
MESH = pl.DeviceIdType.MESH
ORDER = (1, 0, 2)
VMEM_LIMIT = 56 * 1024 * 1024


def far_first(index, count, step):
    half = count // 2
    side, local = index // half, index % half
    side = jnp.where(step < half, 1 - side, side)
    return side * half + (local + step) % half


def kernel(
    row_count, col_count, a_hbm, p_ref, ac_ref, pc_ref, sl_ref, out_ref,
    a_vm, chain, a_high, a_low, following, send, send_cols, recv, recv_cols, dense, rt, prod,
    pair_send, pair_recv, kept, line_send, combo, line_recv,
    a_sem, tile_ss, tile_rs, cols_ss, cols_rs, pair_ss, pair_rs, line_ss, combo_rs, line_rs,
):
    g, c = lax.axis_index("row"), lax.axis_index("col")
    chips = col_count // 2
    z, k = c // 2, c % 2
    own, slots = ac_ref.shape
    bs = p_ref.shape[-1]
    ghosts = 3 * col_count
    wide = CG * bs
    piece = wide // col_count
    half = wide // 2
    couple = z // 2
    buddy = z + 1 - 2 * (z % 2)
    f32, bf16 = jnp.float32, jnp.bfloat16

    def group_ok(group):
        return (group >= 0) & (group < row_count)

    a_copy = pltpu.make_async_copy(a_hbm, a_vm, a_sem)
    barrier = pltpu.get_barrier_semaphore()

    @pl.loop(0, col_count)
    def _(other):
        for t in range(3):
            group = g + 1 - t

            @pl.when(group_ok(group) & ((other != c) | (t != 1)))
            def _():
                pl.semaphore_signal(barrier, inc=1, device_id=(group, other), device_id_type=MESH)

    a_copy.start()

    def pattern(r):
        lane = lax.broadcasted_iota(jnp.int32, (1, 2 * bs), 1)
        return jnp.where(lane < bs, pc_ref[0, r], pc_ref[1, r])

    @pl.loop(0, col_count)
    def _(other):
        for t in range(3):
            j = other * 3 + t
            r = sl_ref[0, j]
            send[j, 0] = p_ref[r, 0]
            send[j, 1] = p_ref[r, 1]
            send_cols[j] = pattern(r)

    peers = col_count - 1
    peers = peers + jnp.where(g > 0, col_count, 0) + jnp.where(g < row_count - 1, col_count, 0)
    pl.semaphore_wait(barrier, peers)

    def tiles_copy(source, target, group, other):
        return pltpu.make_async_remote_copy(
            src_ref=send.at[source], dst_ref=recv.at[target],
            send_sem=tile_ss.at[source], recv_sem=tile_rs.at[target],
            device_id=(group, other), device_id_type=MESH,
        )

    def cols_copy(source, target, group, other):
        return pltpu.make_async_remote_copy(
            src_ref=send_cols.at[source], dst_ref=recv_cols.at[target],
            send_sem=cols_ss.at[source], recv_sem=cols_rs.at[target],
            device_id=(group, other), device_id_type=MESH,
        )

    def pair_copy(w):
        return pltpu.make_async_remote_copy(
            src_ref=pair_send.at[w], dst_ref=pair_recv.at[w],
            send_sem=pair_ss.at[w], recv_sem=pair_rs.at[w],
            device_id=(g, 2 * z + 1 - k), device_id_type=MESH,
        )

    def line_copy(w, block, target, other):
        return pltpu.make_async_remote_copy(
            src_ref=line_send.at[w, block], dst_ref=line_recv.at[w, target],
            send_sem=line_ss.at[w, block], recv_sem=line_rs.at[w, target],
            device_id=(g, 2 * other + k), device_id_type=MESH,
        )

    def combo_copy(w, block):
        return pltpu.make_async_remote_copy(
            src_ref=line_send.at[w, block], dst_ref=combo.at[w, block],
            send_sem=line_ss.at[w, block], recv_sem=combo_rs.at[w, block],
            device_id=(g, 2 * buddy + k), device_id_type=MESH,
        )

    def start_stream(t):
        group = g + 1 - t

        @pl.loop(0, col_count)
        def _(step):
            other = far_first(c, col_count, step)

            @pl.when(group_ok(group) & ((other != c) | (t != 1)))
            def _():
                cols_copy(other * 3 + t, c * 3 + t, group, other).start()
                tiles_copy(other * 3 + t, c * 3 + t, group, other).start()

    def finish_stream(t):
        group = g + 1 - t

        @pl.loop(0, col_count)
        def _(other):
            slot = other * 3 + t

            @pl.when(group_ok(group) & ((other != c) | (t != 1)))
            def _():
                cols_copy(slot, slot, group, other).wait_send()
                tiles_copy(slot, slot, group, other).wait_send()

    for t in ORDER:
        start_stream(t)

    def spread(target, tiles, cols):
        first, second = tiles[0].astype(f32), tiles[1].astype(f32)
        for m in range(CG):
            in_first = jnp.where(cols[:, :bs] == m, 1.0, 0.0)
            in_second = jnp.where(cols[:, bs:] == m, 1.0, 0.0)
            dense[pl.ds(pl.multiple_of(target * bs, bs), bs), m * bs : (m + 1) * bs] = (
                first * in_first + second * in_second
            ).astype(bf16)

    owners = col_count // CG

    @pl.loop(0, own)
    def _(r):
        spread(col_count + r, p_ref.at[r], pattern(r))
        first = p_ref[r, 0].astype(f32).T
        second = p_ref[r, 1].astype(f32).T
        for m in range(CG):
            in_first = jnp.where(pc_ref[0, r] == m, 1.0, 0.0)
            in_second = jnp.where(pc_ref[1, r] == m, 1.0, 0.0)
            block = (first * in_first + second * in_second).astype(bf16)
            for u in range(owners):
                start = (u % 2) * half + (m * (owners // 2) + u // 2) * piece
                rt[start : start + piece, pl.ds(pl.multiple_of(r * bs, bs), bs)] = block[
                    u * piece : (u + 1) * piece
                ]

    def take_stream(t):
        @pl.loop(0, col_count)
        def _(other):
            slot = other * 3 + t

            @pl.when(group_ok(g + t - 1) & ((other != c) | (t != 1)))
            def _():
                cols_copy(slot, slot, g + t - 1, other).wait_recv()
                tiles_copy(slot, slot, g + t - 1, other).wait_recv()
                spread(other, recv.at[slot], recv_cols[slot])

            if t == 1:

                @pl.when(other == c)
                def _():
                    spread(other, send.at[slot], send_cols[slot])

    @pl.loop(0, own)
    def _(i):
        for s in range(slots):
            after = jnp.int32(slots)
            for later in range(slots - 1, s, -1):
                after = jnp.where(ac_ref[i, later] == ac_ref[i, s], later, after)
            following[i, s] = after

    chain[slots] = jnp.zeros((bs, bs), f32)

    def lay_out(t):
        @pl.loop(0, own)
        def _(i):
            for s in range(slots - 1, -1, -1):
                chain[s] = a_vm[i, s].astype(f32) + chain[following[i, s]]
            rows = pl.ds(pl.multiple_of(i * bs, bs), bs)

            def place(position, b):
                first = jnp.int32(slots)
                for s in range(slots - 1, -1, -1):
                    first = jnp.where(ac_ref[i, s] == b, s, first)
                columns = pl.ds(pl.multiple_of(position * bs, bs), bs)
                total = chain[first]
                high = total.astype(bf16)
                a_high[t % a_high.shape[0], rows, columns] = high
                a_low[t % a_low.shape[0], rows, columns] = (total - high.astype(f32)).astype(bf16)

            @pl.loop(0, col_count)
            def _(q):
                place(q, own + 3 * q + t)

            if t == 1:

                @pl.loop(0, own)
                def _(r):
                    place(col_count + r, r)

    def products(w, low, high):
        step_rows = 2 * bs
        depth = (col_count + (own if w == 1 else 0)) * bs

        @pl.loop(low, high)
        def _(step):
            rows = pl.ds(pl.multiple_of(step * step_rows, step_rows), step_rows)
            right = dense[:depth, :]
            total = jnp.dot(a_high[w % a_high.shape[0], rows, :depth], right, preferred_element_type=f32)
            total = total + jnp.dot(a_low[w % a_low.shape[0], rows, :depth], right, preferred_element_type=f32)
            prod[rows, :] = total.astype(bf16)

    def restrict(core):
        rows = rt[pl.ds(pl.multiple_of(core * half, half), half), :]
        return jnp.dot(rows, prod[...], preferred_element_type=f32)

    def block_rows(other):
        return pl.ds(pl.multiple_of(other * piece, piece), piece)

    def beyond_buddy(other):
        return jnp.where(z % 2 == 0, other > z + 1, other < z - 1)

    def beyond_self(other):
        return jnp.where(z % 2 == 0, other < z, other > z)

    def give(w):
        pair_copy(w).wait_recv()
        kept[w] = kept[w] + pair_recv[w]
        out_ref[:, w * wide : (w + 1) * wide] = kept[w, block_rows(z)]

        @pl.loop(0, chips)
        def _(step):
            other = far_first(z, chips, step)

            @pl.when(beyond_buddy(other))
            def _():
                line_send[w, other] = kept[w, block_rows(other)].astype(bf16)
                combo_copy(w, other).start()

        line_send[w, buddy] = kept[w, block_rows(buddy)].astype(bf16)
        line_copy(w, buddy, couple, buddy).start()

    def give_straight(w):
        pair_copy(w).wait_recv()

        @pl.loop(0, chips)
        def _(step):
            other = far_first(z, chips, step)

            @pl.when(other != z)
            def _():
                total = kept[w, block_rows(other)] + pair_recv[w, block_rows(other)]
                line_send[w, other] = total.astype(bf16)
                line_copy(w, other, z, other).start()

        out_ref[:, w * wide : (w + 1) * wide] = (
            kept[w, block_rows(z)] + pair_recv[w, block_rows(z)]
        )

    def pass_on(w):
        @pl.loop(0, chips)
        def _(step):
            other = far_first(z, chips, step)

            @pl.when(beyond_self(other))
            def _():
                combo_copy(w, other).wait_recv()
                total = kept[w, block_rows(other)] + combo[w, other].astype(f32)
                line_send[w, other] = total.astype(bf16)
                line_copy(w, other, couple, other).start()

    a_copy.wait()
    roomy = a_high.shape[0] == 3
    for w in ORDER if roomy else ORDER[:1]:
        lay_out(w)
    steps = own // 2
    for n, w in enumerate(ORDER):
        take_stream(w)
        if n < 2:
            products(w, 0, steps)
        else:
            pass_on(ORDER[0])
            give(ORDER[1])
            products(w, 0, steps // 2)
            pass_on(ORDER[1])
            products(w, steps // 2, steps)
        pair_send[w] = restrict(1 - k)
        pair_copy(w).start()
        kept[w] = restrict(k)
        if n < 2 and not roomy:
            lay_out(ORDER[n + 1])
        if n == 1:
            give(ORDER[0])
    give_straight(ORDER[2])

    for n, w in enumerate(ORDER):
        columns = slice(w * wide, (w + 1) * wide)

        @pl.loop(0, chips // 2 if n < 2 else chips - 1)
        def _(step):
            source = step if n < 2 else (z + 1 + step) % chips
            line_copy(w, buddy, source, buddy).wait_recv()
            out_ref[:, columns] += line_recv[w, source].astype(f32)

        @pl.loop(1, chips)
        def _(step):
            line_copy(w, (z + step) % chips, couple, buddy).wait_send()

        finish_stream(w)
        pair_copy(w).wait_send()


def body(row_count, col_count, a_tiles, a_cols, p_tiles, p_cols, send_list):
    own, slots = a_cols.shape
    tiles = p_cols.shape[1]
    bs = a_tiles.shape[-1]
    ghosts = 3 * col_count
    chips = col_count // 2
    wide = CG * bs
    piece = wide // col_count
    layouts = 3 if col_count <= own else 1
    vmem = pl.BlockSpec(memory_space=pltpu.VMEM)
    smem = pl.BlockSpec(memory_space=pltpu.SMEM)
    dma = pltpu.SemaphoreType.DMA
    f32, bf16 = jnp.float32, jnp.bfloat16
    return pl.pallas_call(
        functools.partial(kernel, row_count, col_count),
        out_shape=jax.ShapeDtypeStruct((piece, 3 * wide), f32),
        in_specs=[pl.BlockSpec(memory_space=pl.ANY), vmem, smem, smem, smem],
        out_specs=vmem,
        scratch_shapes=[
            pltpu.VMEM((own, slots, bs, bs), bf16),
            pltpu.VMEM((slots + 1, bs, bs), f32),
            pltpu.VMEM((layouts, own * bs, (col_count + own) * bs), bf16),
            pltpu.VMEM((layouts, own * bs, (col_count + own) * bs), bf16),
            pltpu.SMEM((own, slots), jnp.int32),
            pltpu.VMEM((ghosts, tiles, bs, bs), bf16),
            pltpu.VMEM((ghosts, 1, tiles * bs), jnp.int32),
            pltpu.VMEM((ghosts, tiles, bs, bs), bf16),
            pltpu.VMEM((ghosts, 1, tiles * bs), jnp.int32),
            pltpu.VMEM(((col_count + own) * bs, wide), bf16),
            pltpu.VMEM((wide, own * bs), bf16),
            pltpu.VMEM((own * bs, wide), bf16),
            pltpu.VMEM((3, wide // 2, wide), f32),
            pltpu.VMEM((3, wide // 2, wide), f32),
            pltpu.VMEM((3, wide // 2, wide), f32),
            pltpu.VMEM((3, chips, piece, wide), bf16),
            pltpu.VMEM((3, chips, piece, wide), bf16),
            pltpu.VMEM((3, chips, piece, wide), bf16),
            dma,
            dma((ghosts,)), dma((ghosts,)), dma((ghosts,)), dma((ghosts,)),
            dma((3,)), dma((3,)), dma((3, chips)), dma((3, chips)), dma((3, chips)),
        ],
        compiler_params=pltpu.CompilerParams(
            collective_id=0, has_side_effects=True, vmem_limit_bytes=VMEM_LIMIT
        ),
        name="triple_product",
    )(a_tiles, p_tiles, a_cols, p_cols.T, send_list)


def solution(mesh):
    in_specs = (
        P(("row", "col"), None, None, None),
        P(("row", "col"), None),
        P(("row", "col"), None, None, None),
        P(("row", "col"), None),
        P(("row", "col"), None),
    )
    out_specs = P(("row", "col"), None)
    return jax.shard_map(
        functools.partial(body, mesh.shape["row"], mesh.shape["col"]),
        mesh=mesh, in_specs=in_specs, out_specs=out_specs, check_vma=False,
    )
```

```python
import functools

import jax
import jax.numpy as jnp
from jax import lax
from jax.experimental import pallas as pl
from jax.experimental.pallas import tpu as pltpu
from jax.sharding import PartitionSpec as P

CG = 4
MESH = pl.DeviceIdType.MESH
ORDER = (1, 0, 2)
VMEM_LIMIT = 56 * 1024 * 1024


def far_first(index, count, step):
    half = count // 2
    side, local = index // half, index % half
    side = jnp.where(step < half, 1 - side, side)
    return side * half + (local + step) % half


def kernel(
    row_count, col_count, a_hbm, p_ref, ac_ref, pc_ref, sl_ref, out_ref,
    a_vm, chain, a_high, a_low, following, send, send_cols, recv, recv_cols, dense, rt, prod,
    pair_send, pair_recv, kept, line_send, combo, line_recv,
    a_sem, tile_ss, tile_rs, cols_ss, cols_rs, pair_ss, pair_rs, line_ss, combo_rs, line_rs,
):
    g, c = lax.axis_index("row"), lax.axis_index("col")
    chips = col_count // 2
    z, k = c // 2, c % 2
    own, slots = ac_ref.shape
    bs = p_ref.shape[-1]
    ghosts = 3 * col_count
    wide = CG * bs
    piece = wide // col_count
    half = wide // 2
    couple = z // 2
    buddy = z + 1 - 2 * (z % 2)
    f32, bf16 = jnp.float32, jnp.bfloat16

    def group_ok(group):
        return (group >= 0) & (group < row_count)

    a_copy = pltpu.make_async_copy(a_hbm, a_vm, a_sem)
    barrier = pltpu.get_barrier_semaphore()

    @pl.loop(0, col_count)
    def _(other):
        for t in range(3):
            group = g + 1 - t

            @pl.when(group_ok(group) & ((other != c) | (t != 1)))
            def _():
                pl.semaphore_signal(barrier, inc=1, device_id=(group, other), device_id_type=MESH)

    a_copy.start()

    def pattern(r):
        lane = lax.broadcasted_iota(jnp.int32, (1, 2 * bs), 1)
        return jnp.where(lane < bs, pc_ref[0, r], pc_ref[1, r])

    def gather(t):
        @pl.loop(0, col_count)
        def _(other):
            j = other * 3 + t
            r = sl_ref[0, j]
            send[j, 0] = p_ref[r, 0]
            send[j, 1] = p_ref[r, 1]
            send_cols[j] = pattern(r)

    gather(ORDER[0])
    peers = col_count - 1
    peers = peers + jnp.where(g > 0, col_count, 0) + jnp.where(g < row_count - 1, col_count, 0)
    pl.semaphore_wait(barrier, peers)

    def tiles_copy(source, target, group, other):
        return pltpu.make_async_remote_copy(
            src_ref=send.at[source], dst_ref=recv.at[target],
            send_sem=tile_ss.at[source], recv_sem=tile_rs.at[target],
            device_id=(group, other), device_id_type=MESH,
        )

    def cols_copy(source, target, group, other):
        return pltpu.make_async_remote_copy(
            src_ref=send_cols.at[source], dst_ref=recv_cols.at[target],
            send_sem=cols_ss.at[source], recv_sem=cols_rs.at[target],
            device_id=(group, other), device_id_type=MESH,
        )

    def pair_copy(w):
        return pltpu.make_async_remote_copy(
            src_ref=pair_send.at[w], dst_ref=pair_recv.at[w],
            send_sem=pair_ss.at[w], recv_sem=pair_rs.at[w],
            device_id=(g, 2 * z + 1 - k), device_id_type=MESH,
        )

    def line_copy(w, block, target, other):
        return pltpu.make_async_remote_copy(
            src_ref=line_send.at[w, block], dst_ref=line_recv.at[w, target],
            send_sem=line_ss.at[w, block], recv_sem=line_rs.at[w, target],
            device_id=(g, 2 * other + k), device_id_type=MESH,
        )

    def combo_copy(w, block):
        return pltpu.make_async_remote_copy(
            src_ref=line_send.at[w, block], dst_ref=combo.at[w, block],
            send_sem=line_ss.at[w, block], recv_sem=combo_rs.at[w, block],
            device_id=(g, 2 * buddy + k), device_id_type=MESH,
        )

    def start_stream(t):
        group = g + 1 - t

        @pl.loop(0, col_count)
        def _(step):
            other = far_first(c, col_count, step)

            @pl.when(group_ok(group) & ((other != c) | (t != 1)))
            def _():
                cols_copy(other * 3 + t, c * 3 + t, group, other).start()
                tiles_copy(other * 3 + t, c * 3 + t, group, other).start()

    def finish_stream(t):
        group = g + 1 - t

        @pl.loop(0, col_count)
        def _(other):
            slot = other * 3 + t

            @pl.when(group_ok(group) & ((other != c) | (t != 1)))
            def _():
                cols_copy(slot, slot, group, other).wait_send()
                tiles_copy(slot, slot, group, other).wait_send()

    for n, t in enumerate(ORDER):
        if n > 0:
            gather(t)
        start_stream(t)

    def spread(target, tiles, cols):
        first, second = tiles[0].astype(f32), tiles[1].astype(f32)
        for m in range(CG):
            in_first = jnp.where(cols[:, :bs] == m, 1.0, 0.0)
            in_second = jnp.where(cols[:, bs:] == m, 1.0, 0.0)
            dense[pl.ds(pl.multiple_of(target * bs, bs), bs), m * bs : (m + 1) * bs] = (
                first * in_first + second * in_second
            ).astype(bf16)

    owners = col_count // CG

    @pl.loop(0, own)
    def _(r):
        spread(col_count + r, p_ref.at[r], pattern(r))
        first = p_ref[r, 0].astype(f32).T
        second = p_ref[r, 1].astype(f32).T
        for m in range(CG):
            in_first = jnp.where(pc_ref[0, r] == m, 1.0, 0.0)
            in_second = jnp.where(pc_ref[1, r] == m, 1.0, 0.0)
            block = (first * in_first + second * in_second).astype(bf16)
            for u in range(owners):
                start = (u % 2) * half + (m * (owners // 2) + u // 2) * piece
                rt[start : start + piece, pl.ds(pl.multiple_of(r * bs, bs), bs)] = block[
                    u * piece : (u + 1) * piece
                ]

    def take_stream(t):
        @pl.loop(0, col_count)
        def _(other):
            slot = other * 3 + t

            @pl.when(group_ok(g + t - 1) & ((other != c) | (t != 1)))
            def _():
                cols_copy(slot, slot, g + t - 1, other).wait_recv()
                tiles_copy(slot, slot, g + t - 1, other).wait_recv()
                spread(other, recv.at[slot], recv_cols[slot])

            if t == 1:

                @pl.when(other == c)
                def _():
                    spread(other, send.at[slot], send_cols[slot])

    @pl.loop(0, own)
    def _(i):
        for s in range(slots):
            after = jnp.int32(slots)
            for later in range(slots - 1, s, -1):
                after = jnp.where(ac_ref[i, later] == ac_ref[i, s], later, after)
            following[i, s] = after

    chain[slots] = jnp.zeros((bs, bs), f32)

    def lay_out(t):
        @pl.loop(0, own)
        def _(i):
            for s in range(slots - 1, -1, -1):
                chain[s] = a_vm[i, s].astype(f32) + chain[following[i, s]]
            rows = pl.ds(pl.multiple_of(i * bs, bs), bs)

            def place(position, b):
                first = jnp.int32(slots)
                for s in range(slots - 1, -1, -1):
                    first = jnp.where(ac_ref[i, s] == b, s, first)
                columns = pl.ds(pl.multiple_of(position * bs, bs), bs)
                total = chain[first]
                high = total.astype(bf16)
                a_high[t % a_high.shape[0], rows, columns] = high
                a_low[t % a_low.shape[0], rows, columns] = (total - high.astype(f32)).astype(bf16)

            @pl.loop(0, col_count)
            def _(q):
                place(q, own + 3 * q + t)

            if t == 1:

                @pl.loop(0, own)
                def _(r):
                    place(col_count + r, r)

    def products(w, low, high):
        step_rows = 2 * bs
        depth = (col_count + (own if w == 1 else 0)) * bs

        @pl.loop(low, high)
        def _(step):
            rows = pl.ds(pl.multiple_of(step * step_rows, step_rows), step_rows)
            right = dense[:depth, :]
            total = jnp.dot(a_high[w % a_high.shape[0], rows, :depth], right, preferred_element_type=f32)
            total = total + jnp.dot(a_low[w % a_low.shape[0], rows, :depth], right, preferred_element_type=f32)
            prod[rows, :] = total.astype(bf16)

    def restrict(core):
        rows = rt[pl.ds(pl.multiple_of(core * half, half), half), :]
        return jnp.dot(rows, prod[...], preferred_element_type=f32)

    def block_rows(other):
        return pl.ds(pl.multiple_of(other * piece, piece), piece)

    def beyond_buddy(other):
        return jnp.where(z % 2 == 0, other > z + 1, other < z - 1)

    def beyond_self(other):
        return jnp.where(z % 2 == 0, other < z, other > z)

    def give(w):
        pair_copy(w).wait_recv()
        kept[w] = kept[w] + pair_recv[w]
        out_ref[:, w * wide : (w + 1) * wide] = kept[w, block_rows(z)]

        @pl.loop(0, chips)
        def _(step):
            other = far_first(z, chips, step)

            @pl.when(beyond_buddy(other))
            def _():
                line_send[w, other] = kept[w, block_rows(other)].astype(bf16)
                combo_copy(w, other).start()

        line_send[w, buddy] = kept[w, block_rows(buddy)].astype(bf16)
        line_copy(w, buddy, couple, buddy).start()

    def give_straight(w):
        pair_copy(w).wait_recv()

        @pl.loop(0, chips)
        def _(step):
            other = far_first(z, chips, step)

            @pl.when(other != z)
            def _():
                total = kept[w, block_rows(other)] + pair_recv[w, block_rows(other)]
                line_send[w, other] = total.astype(bf16)
                line_copy(w, other, z, other).start()

        out_ref[:, w * wide : (w + 1) * wide] = (
            kept[w, block_rows(z)] + pair_recv[w, block_rows(z)]
        )

    def pass_on(w):
        @pl.loop(0, chips)
        def _(step):
            other = far_first(z, chips, step)

            @pl.when(beyond_self(other))
            def _():
                combo_copy(w, other).wait_recv()
                total = kept[w, block_rows(other)] + combo[w, other].astype(f32)
                line_send[w, other] = total.astype(bf16)
                line_copy(w, other, couple, other).start()

    a_copy.wait()
    roomy = a_high.shape[0] == 3
    for w in ORDER if roomy else ORDER[:1]:
        lay_out(w)
    steps = own // 2
    for n, w in enumerate(ORDER):
        take_stream(w)
        if n < 2:
            products(w, 0, steps)
        else:
            products(w, 0, steps // 2)
            pass_on(ORDER[1])
            products(w, steps // 2, steps)
        pair_send[w] = restrict(1 - k)
        pair_copy(w).start()
        kept[w] = restrict(k)
        if n < 2 and not roomy:
            lay_out(ORDER[n + 1])
        if n == 1:
            give(ORDER[0])
            give(ORDER[1])
            pass_on(ORDER[0])
    give_straight(ORDER[2])

    for n, w in enumerate(ORDER):
        columns = slice(w * wide, (w + 1) * wide)

        @pl.loop(0, chips // 2 if n < 2 else chips - 1)
        def _(step):
            source = step if n < 2 else (z + 1 + step) % chips
            line_copy(w, buddy, source, buddy).wait_recv()
            out_ref[:, columns] += line_recv[w, source].astype(f32)

        @pl.loop(1, chips)
        def _(step):
            line_copy(w, (z + step) % chips, couple, buddy).wait_send()

        finish_stream(w)
        pair_copy(w).wait_send()


def body(row_count, col_count, a_tiles, a_cols, p_tiles, p_cols, send_list):
    own, slots = a_cols.shape
    tiles = p_cols.shape[1]
    bs = a_tiles.shape[-1]
    ghosts = 3 * col_count
    chips = col_count // 2
    wide = CG * bs
    piece = wide // col_count
    layouts = 3 if col_count <= own else 1
    vmem = pl.BlockSpec(memory_space=pltpu.VMEM)
    smem = pl.BlockSpec(memory_space=pltpu.SMEM)
    dma = pltpu.SemaphoreType.DMA
    f32, bf16 = jnp.float32, jnp.bfloat16
    return pl.pallas_call(
        functools.partial(kernel, row_count, col_count),
        out_shape=jax.ShapeDtypeStruct((piece, 3 * wide), f32),
        in_specs=[pl.BlockSpec(memory_space=pl.ANY), vmem, smem, smem, smem],
        out_specs=vmem,
        scratch_shapes=[
            pltpu.VMEM((own, slots, bs, bs), bf16),
            pltpu.VMEM((slots + 1, bs, bs), f32),
            pltpu.VMEM((layouts, own * bs, (col_count + own) * bs), bf16),
            pltpu.VMEM((layouts, own * bs, (col_count + own) * bs), bf16),
            pltpu.SMEM((own, slots), jnp.int32),
            pltpu.VMEM((ghosts, tiles, bs, bs), bf16),
            pltpu.VMEM((ghosts, 1, tiles * bs), jnp.int32),
            pltpu.VMEM((ghosts, tiles, bs, bs), bf16),
            pltpu.VMEM((ghosts, 1, tiles * bs), jnp.int32),
            pltpu.VMEM(((col_count + own) * bs, wide), bf16),
            pltpu.VMEM((wide, own * bs), bf16),
            pltpu.VMEM((own * bs, wide), bf16),
            pltpu.VMEM((3, wide // 2, wide), f32),
            pltpu.VMEM((3, wide // 2, wide), f32),
            pltpu.VMEM((3, wide // 2, wide), f32),
            pltpu.VMEM((3, chips, piece, wide), bf16),
            pltpu.VMEM((3, chips, piece, wide), bf16),
            pltpu.VMEM((3, chips, piece, wide), bf16),
            dma,
            dma((ghosts,)), dma((ghosts,)), dma((ghosts,)), dma((ghosts,)),
            dma((3,)), dma((3,)), dma((3, chips)), dma((3, chips)), dma((3, chips)),
        ],
        compiler_params=pltpu.CompilerParams(
            collective_id=0, has_side_effects=True, vmem_limit_bytes=VMEM_LIMIT
        ),
        name="triple_product",
    )(a_tiles, p_tiles, a_cols, p_cols.T, send_list)


def solution(mesh):
    in_specs = (
        P(("row", "col"), None, None, None),
        P(("row", "col"), None),
        P(("row", "col"), None, None, None),
        P(("row", "col"), None),
        P(("row", "col"), None),
    )
    out_specs = P(("row", "col"), None)
    return jax.shard_map(
        functools.partial(body, mesh.shape["row"], mesh.shape["col"]),
        mesh=mesh, in_specs=in_specs, out_specs=out_specs, check_vma=False,
    )
```

```python
import functools

import jax
import jax.numpy as jnp
from jax import lax
from jax.experimental import pallas as pl
from jax.experimental.pallas import tpu as pltpu
from jax.sharding import PartitionSpec as P

CG = 4
MESH = pl.DeviceIdType.MESH
ORDER = (1, 0, 2)
VMEM_LIMIT = 56 * 1024 * 1024


def far_first(index, count, step):
    half = count // 2
    side, local = index // half, index % half
    side = jnp.where(step < half, 1 - side, side)
    return side * half + (local + step) % half


def kernel(
    row_count, col_count, a_hbm, p_ref, ac_ref, pc_ref, sl_ref, out_ref,
    a_vm, chain, chain_high, chain_low, a_high, a_low, following, send, send_cols, recv, recv_cols, dense, rt, prod,
    pair_send, pair_recv, kept, line_send, combo, line_recv,
    a_sem, tile_ss, tile_rs, cols_ss, cols_rs, pair_ss, pair_rs, line_ss, combo_rs, line_rs,
):
    g, c = lax.axis_index("row"), lax.axis_index("col")
    chips = col_count // 2
    z, k = c // 2, c % 2
    own, slots = ac_ref.shape
    bs = p_ref.shape[-1]
    ghosts = 3 * col_count
    wide = CG * bs
    piece = wide // col_count
    half = wide // 2
    couple = z // 2
    buddy = z + 1 - 2 * (z % 2)
    f32, bf16 = jnp.float32, jnp.bfloat16

    def group_ok(group):
        return (group >= 0) & (group < row_count)

    a_copy = pltpu.make_async_copy(a_hbm, a_vm, a_sem)
    barrier = pltpu.get_barrier_semaphore()

    @pl.loop(0, col_count)
    def _(other):
        for t in range(3):
            group = g + 1 - t

            @pl.when(group_ok(group) & ((other != c) | (t != 1)))
            def _():
                pl.semaphore_signal(barrier, inc=1, device_id=(group, other), device_id_type=MESH)

    a_copy.start()

    def pattern(r):
        lane = lax.broadcasted_iota(jnp.int32, (1, 2 * bs), 1)
        return jnp.where(lane < bs, pc_ref[0, r], pc_ref[1, r])

    def gather(t):
        @pl.loop(0, col_count)
        def _(other):
            j = other * 3 + t
            r = sl_ref[0, j]
            send[j, 0] = p_ref[r, 0]
            send[j, 1] = p_ref[r, 1]
            send_cols[j] = pattern(r)

    gather(ORDER[0])
    peers = col_count - 1
    peers = peers + jnp.where(g > 0, col_count, 0) + jnp.where(g < row_count - 1, col_count, 0)
    pl.semaphore_wait(barrier, peers)

    def tiles_copy(source, target, group, other):
        return pltpu.make_async_remote_copy(
            src_ref=send.at[source], dst_ref=recv.at[target],
            send_sem=tile_ss.at[source], recv_sem=tile_rs.at[target],
            device_id=(group, other), device_id_type=MESH,
        )

    def cols_copy(source, target, group, other):
        return pltpu.make_async_remote_copy(
            src_ref=send_cols.at[source], dst_ref=recv_cols.at[target],
            send_sem=cols_ss.at[source], recv_sem=cols_rs.at[target],
            device_id=(group, other), device_id_type=MESH,
        )

    def pair_copy(w):
        return pltpu.make_async_remote_copy(
            src_ref=pair_send.at[w], dst_ref=pair_recv.at[w],
            send_sem=pair_ss.at[w], recv_sem=pair_rs.at[w],
            device_id=(g, 2 * z + 1 - k), device_id_type=MESH,
        )

    def line_copy(w, block, target, other):
        return pltpu.make_async_remote_copy(
            src_ref=line_send.at[w, block], dst_ref=line_recv.at[w, target],
            send_sem=line_ss.at[w, block], recv_sem=line_rs.at[w, target],
            device_id=(g, 2 * other + k), device_id_type=MESH,
        )

    def combo_copy(w, block):
        return pltpu.make_async_remote_copy(
            src_ref=line_send.at[w, block], dst_ref=combo.at[w, block],
            send_sem=line_ss.at[w, block], recv_sem=combo_rs.at[w, block],
            device_id=(g, 2 * buddy + k), device_id_type=MESH,
        )

    def start_stream(t):
        group = g + 1 - t

        @pl.loop(0, col_count)
        def _(step):
            other = far_first(c, col_count, step)

            @pl.when(group_ok(group) & ((other != c) | (t != 1)))
            def _():
                cols_copy(other * 3 + t, c * 3 + t, group, other).start()
                tiles_copy(other * 3 + t, c * 3 + t, group, other).start()

    def finish_stream(t):
        group = g + 1 - t

        @pl.loop(0, col_count)
        def _(other):
            slot = other * 3 + t

            @pl.when(group_ok(group) & ((other != c) | (t != 1)))
            def _():
                cols_copy(slot, slot, group, other).wait_send()
                tiles_copy(slot, slot, group, other).wait_send()

    for n, t in enumerate(ORDER):
        if n > 0:
            gather(t)
        start_stream(t)

    def spread(target, tiles, cols):
        first, second = tiles[0].astype(f32), tiles[1].astype(f32)
        for m in range(CG):
            in_first = jnp.where(cols[:, :bs] == m, 1.0, 0.0)
            in_second = jnp.where(cols[:, bs:] == m, 1.0, 0.0)
            dense[pl.ds(pl.multiple_of(target * bs, bs), bs), m * bs : (m + 1) * bs] = (
                first * in_first + second * in_second
            ).astype(bf16)

    owners = col_count // CG

    @pl.loop(0, own)
    def _(r):
        spread(col_count + r, p_ref.at[r], pattern(r))
        first = p_ref[r, 0].astype(f32).T
        second = p_ref[r, 1].astype(f32).T
        for m in range(CG):
            in_first = jnp.where(pc_ref[0, r] == m, 1.0, 0.0)
            in_second = jnp.where(pc_ref[1, r] == m, 1.0, 0.0)
            block = (first * in_first + second * in_second).astype(bf16)
            for u in range(owners):
                start = (u % 2) * half + (m * (owners // 2) + u // 2) * piece
                rt[start : start + piece, pl.ds(pl.multiple_of(r * bs, bs), bs)] = block[
                    u * piece : (u + 1) * piece
                ]

    def take_stream(t):
        @pl.loop(0, col_count)
        def _(other):
            slot = other * 3 + t

            @pl.when(group_ok(g + t - 1) & ((other != c) | (t != 1)))
            def _():
                cols_copy(slot, slot, g + t - 1, other).wait_recv()
                tiles_copy(slot, slot, g + t - 1, other).wait_recv()
                spread(other, recv.at[slot], recv_cols[slot])

            if t == 1:

                @pl.when(other == c)
                def _():
                    spread(other, send.at[slot], send_cols[slot])

    @pl.loop(0, own)
    def _(i):
        for s in range(slots):
            after = jnp.int32(slots)
            for later in range(slots - 1, s, -1):
                after = jnp.where(ac_ref[i, later] == ac_ref[i, s], later, after)
            following[i, s] = after

    chain[slots] = jnp.zeros((bs, bs), f32)

    chain_high[slots] = jnp.zeros((bs, bs), bf16)
    chain_low[slots] = jnp.zeros((bs, bs), bf16)

    def lay_out(windows):
        @pl.loop(0, own)
        def _(i):
            named = [ac_ref[i, s] for s in range(slots)]
            for s in range(slots - 1, -1, -1):
                total = a_vm[i, s].astype(f32) + chain[following[i, s]]
                high = total.astype(bf16)
                chain[s] = total
                chain_high[s] = high
                chain_low[s] = (total - high.astype(f32)).astype(bf16)
            rows = pl.ds(pl.multiple_of(i * bs, bs), bs)

            def place(at, position, b):
                first = jnp.int32(slots)
                for s in range(slots - 1, -1, -1):
                    first = jnp.where(named[s] == b, s, first)
                columns = slice(position * bs, (position + 1) * bs)
                a_high[at, rows, columns] = chain_high[first]
                a_low[at, rows, columns] = chain_low[first]

            for t in windows:
                at = t % a_high.shape[0]
                for q in range(col_count):
                    place(at, q, own + 3 * q + t)
                if t == 1:
                    for r in range(own):
                        place(at, col_count + r, r)

    def products(w, low, high):
        step_rows = 2 * bs
        depth = (col_count + (own if w == 1 else 0)) * bs

        @pl.loop(low, high)
        def _(step):
            rows = pl.ds(pl.multiple_of(step * step_rows, step_rows), step_rows)
            right = dense[:depth, :]
            total = jnp.dot(a_high[w % a_high.shape[0], rows, :depth], right, preferred_element_type=f32)
            total = total + jnp.dot(a_low[w % a_low.shape[0], rows, :depth], right, preferred_element_type=f32)
            prod[rows, :] = total.astype(bf16)

    def restrict(core):
        rows = rt[pl.ds(pl.multiple_of(core * half, half), half), :]
        return jnp.dot(rows, prod[...], preferred_element_type=f32)

    def block_rows(other):
        return pl.ds(pl.multiple_of(other * piece, piece), piece)

    def beyond_buddy(other):
        return jnp.where(z % 2 == 0, other > z + 1, other < z - 1)

    def beyond_self(other):
        return jnp.where(z % 2 == 0, other < z, other > z)

    def give(w):
        pair_copy(w).wait_recv()
        kept[w] = kept[w] + pair_recv[w]
        out_ref[:, w * wide : (w + 1) * wide] = kept[w, block_rows(z)]

        @pl.loop(0, chips)
        def _(step):
            other = far_first(z, chips, step)

            @pl.when(beyond_buddy(other))
            def _():
                line_send[w, other] = kept[w, block_rows(other)].astype(bf16)
                combo_copy(w, other).start()

        line_send[w, buddy] = kept[w, block_rows(buddy)].astype(bf16)
        line_copy(w, buddy, couple, buddy).start()

    def give_straight(w):
        pair_copy(w).wait_recv()

        @pl.loop(0, chips)
        def _(step):
            other = far_first(z, chips, step)

            @pl.when(other != z)
            def _():
                total = kept[w, block_rows(other)] + pair_recv[w, block_rows(other)]
                line_send[w, other] = total.astype(bf16)
                line_copy(w, other, z, other).start()

        out_ref[:, w * wide : (w + 1) * wide] = (
            kept[w, block_rows(z)] + pair_recv[w, block_rows(z)]
        )

    def pass_on(w):
        @pl.loop(0, chips)
        def _(step):
            other = far_first(z, chips, step)

            @pl.when(beyond_self(other))
            def _():
                combo_copy(w, other).wait_recv()
                total = kept[w, block_rows(other)] + combo[w, other].astype(f32)
                line_send[w, other] = total.astype(bf16)
                line_copy(w, other, couple, other).start()

    a_copy.wait()
    roomy = a_high.shape[0] == 3
    lay_out(ORDER if roomy else ORDER[:1])
    steps = own // 2
    for n, w in enumerate(ORDER):
        take_stream(w)
        if n < 2:
            products(w, 0, steps)
        else:
            products(w, 0, steps // 2)
            pass_on(ORDER[1])
            products(w, steps // 2, steps)
        pair_send[w] = restrict(1 - k)
        pair_copy(w).start()
        kept[w] = restrict(k)
        if n < 2 and not roomy:
            lay_out(ORDER[n + 1 : n + 2])
        if n == 1:
            give(ORDER[0])
            give(ORDER[1])
            pass_on(ORDER[0])
    give_straight(ORDER[2])

    for n, w in enumerate(ORDER):
        columns = slice(w * wide, (w + 1) * wide)

        @pl.loop(0, chips // 2 if n < 2 else chips - 1)
        def _(step):
            source = step if n < 2 else (z + 1 + step) % chips
            line_copy(w, buddy, source, buddy).wait_recv()
            out_ref[:, columns] += line_recv[w, source].astype(f32)

        @pl.loop(1, chips)
        def _(step):
            line_copy(w, (z + step) % chips, couple, buddy).wait_send()

        finish_stream(w)
        pair_copy(w).wait_send()


def body(row_count, col_count, a_tiles, a_cols, p_tiles, p_cols, send_list):
    own, slots = a_cols.shape
    tiles = p_cols.shape[1]
    bs = a_tiles.shape[-1]
    ghosts = 3 * col_count
    chips = col_count // 2
    wide = CG * bs
    piece = wide // col_count
    layouts = 3 if col_count <= own else 1
    vmem = pl.BlockSpec(memory_space=pltpu.VMEM)
    smem = pl.BlockSpec(memory_space=pltpu.SMEM)
    dma = pltpu.SemaphoreType.DMA
    f32, bf16 = jnp.float32, jnp.bfloat16
    return pl.pallas_call(
        functools.partial(kernel, row_count, col_count),
        out_shape=jax.ShapeDtypeStruct((piece, 3 * wide), f32),
        in_specs=[pl.BlockSpec(memory_space=pl.ANY), vmem, smem, smem, smem],
        out_specs=vmem,
        scratch_shapes=[
            pltpu.VMEM((own, slots, bs, bs), bf16),
            pltpu.VMEM((slots + 1, bs, bs), f32),
            pltpu.VMEM((slots + 1, bs, bs), bf16),
            pltpu.VMEM((slots + 1, bs, bs), bf16),
            pltpu.VMEM((layouts, own * bs, (col_count + own) * bs), bf16),
            pltpu.VMEM((layouts, own * bs, (col_count + own) * bs), bf16),
            pltpu.SMEM((own, slots), jnp.int32),
            pltpu.VMEM((ghosts, tiles, bs, bs), bf16),
            pltpu.VMEM((ghosts, 1, tiles * bs), jnp.int32),
            pltpu.VMEM((ghosts, tiles, bs, bs), bf16),
            pltpu.VMEM((ghosts, 1, tiles * bs), jnp.int32),
            pltpu.VMEM(((col_count + own) * bs, wide), bf16),
            pltpu.VMEM((wide, own * bs), bf16),
            pltpu.VMEM((own * bs, wide), bf16),
            pltpu.VMEM((3, wide // 2, wide), f32),
            pltpu.VMEM((3, wide // 2, wide), f32),
            pltpu.VMEM((3, wide // 2, wide), f32),
            pltpu.VMEM((3, chips, piece, wide), bf16),
            pltpu.VMEM((3, chips, piece, wide), bf16),
            pltpu.VMEM((3, chips, piece, wide), bf16),
            dma,
            dma((ghosts,)), dma((ghosts,)), dma((ghosts,)), dma((ghosts,)),
            dma((3,)), dma((3,)), dma((3, chips)), dma((3, chips)), dma((3, chips)),
        ],
        compiler_params=pltpu.CompilerParams(
            collective_id=0, has_side_effects=True, vmem_limit_bytes=VMEM_LIMIT
        ),
        name="triple_product",
    )(a_tiles, p_tiles, a_cols, p_cols.T, send_list)


def solution(mesh):
    in_specs = (
        P(("row", "col"), None, None, None),
        P(("row", "col"), None),
        P(("row", "col"), None, None, None),
        P(("row", "col"), None),
        P(("row", "col"), None),
    )
    out_specs = P(("row", "col"), None)
    return jax.shard_map(
        functools.partial(body, mesh.shape["row"], mesh.shape["col"]),
        mesh=mesh, in_specs=in_specs, out_specs=out_specs, check_vma=False,
    )
```
